256 devices in a mesh: rows: 32 (over z, y), cols: 8 (over x, core).
Axes of the slice: x: 4, y: 4, z: 8, core: 2. Of those that a mesh axis runs over, the one named last changes fastest.
Arguments:
- source_cells: bfloat16 [64, 262144], P(None, 'rows'), may hold values from -21 to 21
- target_cells: bfloat16 [64, 262144], P(None, 'cols'), may hold values from -21 to 21
- source_logmass: float32 [262144], P('rows'), may hold values from -3 to 3
- target_logmass: float32 [262144], P('cols'), may hold values from -3 to 3
- neighbours: int32 [2048, 16], P('rows'), may hold values from 0 to 2047, as said below
Outputs:
- source_potential: float32 [262144], P('rows')
- target_potential: float32 [262144], P('cols')
The draws below stay inside these ranges and needn't reach their ends.
Inputs may be any that keep to these rules, and one draw needn't show every extreme that they name: `neighbours`: each row names 16 distinct target blocks and every target block is named by some row. No row names more than 4 blocks of one range c * 256 to (c + 1) * 256 - 1, and in every draw some rows name exactly 4 of one range; how many entries of a row fall in one range depends only on the row's rows index.
All inputs are finite; a program needn't handle non-finite values.
Results may differ from the reference program's by a relative error of at most 0.0003.
Values sent between devices are 32-bit elements; how exact they have to be, the bound alone decides.
A program may use at most 128 MiB of HBM per device.

```python
import jax
import jax.numpy as jnp
import numpy as np
from jax import lax

DIM = 64
BLOCK = 128
LIST = 16
ITERS = 3
SB_DEV = 64
TB_DEV = 256
NSB = 2048
NTB = 2048
NS = 262144
NT = 262144


def draw_neighbours(key, part):
    key = jax.random.fold_in(key, 5)
    turn_key, perm_key, shuffle_key = jax.random.split(key, 3)
    n_cols = NTB // TB_DEV
    per_shard = LIST // n_cols
    counts = np.full((n_cols,), per_shard)
    counts[0] = 2 * per_shard
    counts[n_cols // 2] = 0
    offset_list = []
    within_list = []
    for shift_by in range(n_cols):
        for place in range(int(counts[shift_by])):
            offset_list.append(shift_by)
            within_list.append(place)
    offsets = jnp.array(offset_list, jnp.int32)
    within = jnp.array(within_list, jnp.int32)
    run_length = jnp.array(counts, jnp.int32)[offsets]
    rotate = jax.random.randint(turn_key, (), 0, n_cols)
    blocks = jnp.arange(NSB, dtype=jnp.int32)
    row_shard = blocks // SB_DEV
    in_shard = blocks % SB_DEV
    home = (row_shard + rotate) % n_cols
    column = (home[:, None] + offsets[None, :]) % n_cols
    position = (row_shard[:, None] * (SB_DEV * per_shard) + in_shard[:, None] * run_length[None, :] + within[None, :]) % TB_DEV

    def table_row(subkey):
        return jax.random.permutation(subkey, TB_DEV).astype(jnp.int32)

    def shuffled(subkey):
        return jax.random.permutation(subkey, LIST).astype(jnp.int32)
    tables = jax.vmap(table_row)(jax.random.split(perm_key, n_cols))
    chosen = column * TB_DEV + tables[column, position]
    shuffles = jax.vmap(shuffled)(jax.random.split(shuffle_key, NSB))
    return jnp.take_along_axis(chosen, shuffles, axis=1).astype(jnp.int32)


def draw_source_cells(key, part):
    key = jax.random.fold_in(key, 17)
    value_key = jax.random.fold_in(key, 0)
    values = jnp.clip(jax.random.normal(value_key, (DIM, NS), jnp.float32), -5.0, 5.0)
    return values.astype(jnp.bfloat16)


def draw_target_cells(key, part):
    key = jax.random.fold_in(key, 23)
    value_key = jax.random.fold_in(key, 0)
    values = jnp.clip(jax.random.normal(value_key, (DIM, NT), jnp.float32), -5.0, 5.0)
    return values.astype(jnp.bfloat16)


def block_levels(stream_key, dims, shards, low, high):
    gain = 1.0
    for axis_at, shards_of in shards:
        draws = jax.random.uniform(jax.random.fold_in(jax.random.fold_in(stream_key, 6), axis_at), (shards_of,), jnp.float32, low / len(shards), high / len(shards))
        gain = gain * jnp.repeat(jnp.exp(draws), dims[axis_at] // shards_of).reshape((-1,) + (1,) * (len(dims) - 1 - axis_at))
    return gain


def setup_inputs(seed: int = 0) -> dict:
    streams_of = jax.random.split(jax.random.key(seed), 6)
    source_cells = draw_source_cells(jax.random.fold_in(streams_of[5], 71), 0)
    target_cells = draw_target_cells(jax.random.fold_in(streams_of[5], 71), 0)
    source_logmass = jnp.clip(jax.random.uniform(streams_of[2], (NS,), jnp.float32, -3.0, 3.0) * block_levels(streams_of[2], (NS,), ((0, 32),), -0.4, 0.0), -3.0, 3.0)
    target_logmass = jnp.clip(jax.random.uniform(streams_of[3], (NT,), jnp.float32, -3.0, 3.0) * block_levels(streams_of[3], (NT,), ((0, 8),), -0.4, 0.0), -3.0, 3.0)
    neighbours = draw_neighbours(jax.random.fold_in(streams_of[5], 71), 0)
    return dict(source_cells=source_cells, target_cells=target_cells, source_logmass=source_logmass, target_logmass=target_logmass, neighbours=neighbours)


EPS = 0.05
NEG = -1.0e30


def reference(source_cells, target_cells, source_logmass, target_logmass, neighbours):
    src_blocks = neighbours.shape[0]
    tgt_blocks = target_cells.shape[1] // BLOCK
    src_three = jnp.moveaxis(source_cells.reshape(DIM, src_blocks, BLOCK), 1, 0)
    tgt_three = target_cells.reshape(DIM, tgt_blocks, BLOCK)
    tgt_squares = jnp.sum(jnp.square(tgt_three.astype(jnp.float32)), axis=0)

    def block_costs(args):
        cells_in, listed = args
        gathered = tgt_three[:, listed, :].reshape(DIM, LIST * BLOCK)
        squares = jnp.sum(jnp.square(cells_in.astype(jnp.float32)), axis=0)
        crossed = jnp.dot(cells_in.T, gathered, preferred_element_type=jnp.float32)
        return ((squares[:, None] + tgt_squares[listed].reshape(1, LIST * BLOCK)) - 2.0 * crossed) / DIM

    costs = lax.map(block_costs, (src_three, neighbours))
    src_mass = source_logmass.reshape(src_blocks, BLOCK)
    tgt_mass = target_logmass.reshape(tgt_blocks, BLOCK)
    flat_ids = neighbours.reshape(-1)
    target_pot = jnp.zeros((tgt_blocks, BLOCK), jnp.float32)
    source_pot = jnp.zeros((src_blocks, BLOCK), jnp.float32)
    for step in range(ITERS):
        def source_rows(args):
            costs_in, listed, log_mass = args
            scores = (target_pot[listed].reshape(1, LIST * BLOCK) - costs_in) / EPS
            highest = jnp.max(scores, axis=1)
            totals = jnp.sum(jnp.exp(scores - highest[:, None]), axis=1)
            return EPS * (log_mass - (highest + jnp.log(totals)))

        source_pot = lax.map(source_rows, (costs, neighbours, src_mass))

        def column_peak(args):
            costs_in, potential = args
            scores = (potential[:, None] - costs_in) / EPS
            return jnp.max(scores, axis=0).reshape(LIST, BLOCK)

        peaks = lax.map(column_peak, (costs, source_pot))
        highest = jnp.full((tgt_blocks, BLOCK), NEG, jnp.float32).at[flat_ids].max(peaks.reshape(-1, BLOCK))

        def column_total(args):
            costs_in, potential, listed = args
            scores = (potential[:, None] - costs_in) / EPS
            shifted = scores - highest[listed].reshape(1, LIST * BLOCK)
            return jnp.sum(jnp.exp(shifted), axis=0).reshape(LIST, BLOCK)

        totals = lax.map(column_total, (costs, source_pot, neighbours))
        summed = jax.ops.segment_sum(totals.reshape(-1, BLOCK), flat_ids, num_segments=tgt_blocks)
        target_pot = EPS * (tgt_mass - (highest + jnp.log(summed)))
    return source_pot.reshape(-1), target_pot.reshape(-1)
```

```python
import functools
import math

import jax
import jax.numpy as jnp
from jax import lax
from jax.experimental import pallas as pl
from jax.experimental.pallas import tpu as pltpu
from jax.sharding import PartitionSpec as P

BLOCK = 128
LIST = 16
ITERS = 3
SLOTS = 4
EPS = 0.05
NEG = -1e30
LOG2E = math.log2(math.e)
UNIT = EPS / LOG2E
CHUNKS = 4
SCAN = (1, 2, 4, 8, 16, 32)
MESH = pl.DeviceIdType.MESH


def log2(v):
    return jnp.log(v) * LOG2E


def kernel(
    n_rows, n_cols, remote,
    ids_ref, trow_ref, tcol_ref, x_ref, y_ref, a_ref, b_ref,
    f_ref, g_ref,
    cells_y, tile, gam, sqx, sqy, hits, first, last, masks, part, src, trg, landing, own,
    y_sem, src_send, src_recv, trg_send, trg_recv, own_send, own_recv,
):
    dim = x_ref.shape[0]
    kappa = 2.0 * LOG2E / (dim * EPS)
    sb, tb = x_ref.shape[1] // BLOCK, y_ref.shape[1] // BLOCK
    pairs = sb * SLOTS
    share = tb // n_rows
    step = sb // CHUNKS
    if remote:
        me_r, me_c = lax.axis_index("rows"), lax.axis_index("cols")
        barrier = pltpu.get_barrier_semaphore()

        @pl.loop(1, n_rows)
        def _(d):
            pl.semaphore_signal(
                barrier, inc=1, device_id={"rows": lax.rem(me_r + d, n_rows)}, device_id_type=MESH
            )

        @pl.loop(1, n_cols)
        def _(d):
            pl.semaphore_signal(
                barrier, inc=1, device_id={"cols": lax.rem(me_c + d, n_cols)}, device_id_type=MESH
            )
    else:
        me_r = me_c = 0

    @pl.loop(0, tb, unroll=8)
    def _(t):
        pltpu.make_async_copy(
            y_ref.at[:, pl.ds(pl.multiple_of(t * BLOCK, BLOCK), BLOCK)], cells_y.at[t], y_sem
        ).start()

    cells_y[tb] = jnp.zeros((dim, BLOCK), jnp.bfloat16)
    pltpu.make_async_copy(cells_y.at[pl.ds(0, tb)], cells_y.at[pl.ds(0, tb)], y_sem).wait()

    @pl.loop(0, tb, unroll=8)
    def _(t):
        cells = cells_y[t].astype(jnp.float32)
        squares = jnp.sum(cells * cells, axis=0, keepdims=True) * (0.5 * kappa)
        sqy[pl.ds(t, 1), :] = squares
        gam[pl.ds(t, 1), :] = -squares

    gam[pl.ds(tb, 8), :] = jnp.full((8, BLOCK), NEG, jnp.float32)

    @pl.loop(0, sb, unroll=8)
    def _(b):
        cells = x_ref[:, pl.ds(pl.multiple_of(b * BLOCK, BLOCK), BLOCK)].astype(jnp.float32)
        sqx[pl.ds(b, 1), :] = jnp.sum(cells * cells, axis=0, keepdims=True) * (0.5 * kappa)

    tr, tc = trow_ref[...], tcol_ref[...]
    ip = lax.broadcasted_iota(jnp.int32, (pairs, pairs), 0)
    iq = lax.broadcasted_iota(jnp.int32, (pairs, pairs), 1)
    before = (tc < tr) | ((tc == tr) & (ip < iq))
    place = jnp.sum(jnp.where(before, 1.0, 0.0), axis=0, keepdims=True)
    put = place == ip.astype(jnp.float32)
    first[...] = jnp.where(put, 1.0, 0.0).astype(jnp.bfloat16)
    trf = tr.astype(jnp.float32)
    ordered = jnp.sum(jnp.where(put, trf, 0.0), axis=1, keepdims=True)
    it_ = lax.broadcasted_iota(jnp.int32, (tb, pairs), 0)
    iu = lax.broadcasted_iota(jnp.int32, (tb, pairs), 1)
    upto = jnp.sum(jnp.where(tr <= it_, 1.0, 0.0), axis=1, keepdims=True)
    count = jnp.sum(jnp.where(tr == it_, 1.0, 0.0), axis=1, keepdims=True)
    at = jnp.where(count > 0.0, upto - 1.0, -1.0)
    last[...] = jnp.where(iu.astype(jnp.float32) == at, 1.0, 0.0).astype(jnp.bfloat16)
    hits[...] = jnp.broadcast_to(jnp.where(count > 0.0, 0.0, NEG), (tb, BLOCK))
    wide = jnp.broadcast_to(ordered, (pairs, BLOCK))
    rows = lax.broadcasted_iota(jnp.int32, (pairs, BLOCK), 0)
    for k, d in enumerate(SCAN):
        same = (wide == pltpu.roll(wide, d, 0)) & (rows >= d)
        masks[k] = jnp.where(same, 0.0, NEG)

    @pl.loop(0, sb)
    def _(b):
        cells = x_ref[:, pl.ds(pl.multiple_of(b * BLOCK, BLOCK), BLOCK)]
        listed = []
        for s in range(SLOTS):
            listed.append(cells_y[ids_ref[b * SLOTS + s]])
        crossed = lax.dot_general(
            cells, jnp.concatenate(listed, axis=1), (((0,), (0,)), ((), ())),
            preferred_element_type=jnp.float32,
        )
        tile[b] = crossed * kappa

    if remote:
        pl.semaphore_wait(barrier, n_rows + n_cols - 2)

    lanes = lax.broadcasted_iota(jnp.int32, (BLOCK, BLOCK), 1)

    def pick(onehot, v):
        high = v.astype(jnp.bfloat16)
        rest = v - high.astype(jnp.float32)
        middle = rest.astype(jnp.bfloat16)
        low = (rest - middle.astype(jnp.float32)).astype(jnp.bfloat16)
        out = jnp.dot(
            onehot, jnp.concatenate([high, middle, low], axis=1), preferred_element_type=jnp.float32
        )
        return (out[:, :BLOCK] + out[:, BLOCK : 2 * BLOCK]) + out[:, 2 * BLOCK :]

    @pl.loop(0, ITERS)
    def _(it):
        for q in range(CHUNKS):

            def source_block(k, acc):
                b = q * step + k
                scores = []
                for s in range(SLOTS):
                    row = gam[ids_ref[b * SLOTS + s]][None, :]
                    scores.append(tile[b, :, s * BLOCK : (s + 1) * BLOCK] + row)
                peak = functools.reduce(jnp.maximum, scores)
                peak = jnp.max(peak, axis=1, keepdims=True)
                total = functools.reduce(jnp.add, [jnp.exp2(v - peak) for v in scores])
                total = jnp.sum(total, axis=1, keepdims=True)
                return jnp.where(lanes == k, peak + log2(total), acc)

            acc = lax.fori_loop(
                0, step, source_block, jnp.zeros((BLOCK, BLOCK), jnp.float32), unroll=2
            )
            src[it, me_c, pl.ds(q * step, step), :] = acc.T[:step, :]
            if remote:

                @pl.loop(1, n_cols)
                def _(d):
                    there = src.at[it, me_c, pl.ds(q * step, step)]
                    pltpu.make_async_remote_copy(
                        src_ref=there, dst_ref=there,
                        send_sem=src_send.at[it], recv_sem=src_recv.at[it, q],
                        device_id={"cols": lax.rem(me_c + d, n_cols)}, device_id_type=MESH,
                    ).start()

        for q in range(CHUNKS):
            if remote:
                landed = src.at[it, pl.ds(0, n_cols - 1), pl.ds(q * step, step)]
                pltpu.make_async_copy(landed, landed, src_recv.at[it, q]).wait()
            parts = src[it, :, pl.ds(q * step, step), :]
            peak = jnp.max(parts, axis=0)
            total = jnp.sum(jnp.exp2(parts - peak[None]), axis=0)
            phi = a_ref[pl.ds(q * step, step), :] * LOG2E - (peak + log2(total))
            f_ref[pl.ds(q * step, step), :] = UNIT * (phi + sqx[pl.ds(q * step, step), :])
            tall = jnp.concatenate([phi, jnp.zeros((BLOCK - step, BLOCK), jnp.float32)], axis=0).T

            @pl.loop(0, step, unroll=2)
            def _(k):
                b = q * step + k
                column = jnp.sum(jnp.where(lanes == k, tall, 0.0), axis=1, keepdims=True)
                for s in range(SLOTS):
                    scores = tile[b, :, s * BLOCK : (s + 1) * BLOCK] + column
                    peak = jnp.max(scores, axis=0, keepdims=True)
                    total = jnp.sum(jnp.exp2(scores - peak), axis=0, keepdims=True)
                    part[pl.ds(b * SLOTS + s, 1), :] = peak + log2(total)

        v = pick(first[...], part[...])
        for k, d in enumerate(SCAN):
            other = pltpu.roll(v, d, 0) + masks[k]
            peak = jnp.maximum(v, other)
            v = peak + log2(1.0 + jnp.exp2(jnp.minimum(v, other) - peak))
        v = pick(last[...], v) + hits[...]
        trg[it, :, :, :] = v.reshape(n_rows, share, BLOCK)
        if remote:

            @pl.loop(1, n_rows)
            def _(d):
                peer = lax.rem(me_r + d, n_rows)
                pltpu.make_async_remote_copy(
                    src_ref=trg.at[it, peer], dst_ref=landing.at[it, me_r],
                    send_sem=trg_send.at[it], recv_sem=trg_recv.at[it],
                    device_id={"rows": peer}, device_id_type=MESH,
                ).start()

        landing[it, me_r] = trg[it, me_r]
        if remote:
            landed = landing.at[it, pl.ds(0, n_rows - 1)]
            pltpu.make_async_copy(landed, landed, trg_recv.at[it]).wait()
        parts = landing[it]
        peak = jnp.max(parts, axis=0)
        total = jnp.sum(jnp.exp2(parts - peak[None]), axis=0)
        mass = b_ref[pl.ds(pl.multiple_of(me_r * share, share), share), :]
        own[it, me_r] = mass * LOG2E - (peak + log2(total))
        if remote:

            @pl.loop(1, n_rows)
            def _(d):
                pltpu.make_async_remote_copy(
                    src_ref=own.at[it, me_r], dst_ref=own.at[it, me_r],
                    send_sem=own_send.at[it], recv_sem=own_recv.at[it],
                    device_id={"rows": lax.rem(me_r + d, n_rows)}, device_id_type=MESH,
                ).start()

            landed = own.at[it, pl.ds(0, n_rows - 1)]
            pltpu.make_async_copy(landed, landed, own_recv.at[it]).wait()
        gam[pl.ds(0, tb), :] = own[it].reshape(tb, BLOCK)

    g_ref[...] = UNIT * (gam[pl.ds(0, tb), :] + sqy[...])
    if remote:
        for it in range(ITERS):
            sent = src.at[it, pl.ds(0, n_cols - 1)]
            pltpu.make_async_copy(sent, sent, src_send.at[it]).wait()
            sent = own.at[it, pl.ds(0, n_rows - 1)]
            pltpu.make_async_copy(sent, sent, own_send.at[it]).wait()
            pltpu.make_async_copy(sent, sent, trg_send.at[it]).wait()


def scratch(n_rows, n_cols, dim, sb, tb):
    f32, pairs = jnp.float32, sb * SLOTS
    dma = pltpu.SemaphoreType.DMA
    return [
        pltpu.VMEM((tb + 1, dim, BLOCK), jnp.bfloat16),
        pltpu.VMEM((sb, BLOCK, SLOTS * BLOCK), f32),
        pltpu.VMEM((tb + 8, BLOCK), f32),
        pltpu.VMEM((sb, BLOCK), f32),
        pltpu.VMEM((tb, BLOCK), f32),
        pltpu.VMEM((tb, BLOCK), f32),
        pltpu.VMEM((pairs, pairs), jnp.bfloat16),
        pltpu.VMEM((tb, pairs), jnp.bfloat16),
        pltpu.VMEM((len(SCAN), pairs, BLOCK), f32),
        pltpu.VMEM((pairs, BLOCK), f32),
        pltpu.VMEM((ITERS, n_cols, sb, BLOCK), f32),
        pltpu.VMEM((ITERS, n_rows, tb // n_rows, BLOCK), f32),
        pltpu.VMEM((ITERS, n_rows, tb // n_rows, BLOCK), f32),
        pltpu.VMEM((ITERS, n_rows, tb // n_rows, BLOCK), f32),
        dma,
        dma((ITERS,)),
        dma((ITERS, CHUNKS)),
        dma((ITERS,)),
        dma((ITERS,)),
        dma((ITERS,)),
        dma((ITERS,)),
    ]


def on_device(n_rows, n_cols, source_cells, target_cells, source_logmass, target_logmass, neighbours):
    sb = neighbours.shape[0]
    tb = target_cells.shape[1] // BLOCK
    pairs = sb * SLOTS
    local = neighbours - lax.axis_index("cols") * tb
    owned = (local >= 0) & (local < tb)
    upto = jnp.arange(LIST)[:, None] <= jnp.arange(LIST)[None, :]
    nth = jnp.sum(jnp.where(owned[:, :, None] & upto[None], 1, 0), axis=1)
    wanted = (nth[:, :, None] == 1 + jnp.arange(SLOTS)[None, None, :]) & owned[:, :, None]
    ids = tb + jnp.sum(jnp.where(wanted, local[:, :, None] - tb, 0), axis=1)
    ids = ids.reshape(pairs).astype(jnp.int32)
    vmem = pl.BlockSpec(memory_space=pltpu.VMEM)
    f, g = pl.pallas_call(
        functools.partial(kernel, n_rows, n_cols, True),
        out_shape=(
            jax.ShapeDtypeStruct((sb, BLOCK), jnp.float32),
            jax.ShapeDtypeStruct((tb, BLOCK), jnp.float32),
        ),
        in_specs=[pl.BlockSpec(memory_space=pltpu.SMEM), vmem, vmem, vmem]
        + [pl.BlockSpec(memory_space=pl.ANY), vmem, vmem],
        out_specs=(vmem, vmem),
        scratch_shapes=scratch(n_rows, n_cols, source_cells.shape[0], sb, tb),
        compiler_params=pltpu.CompilerParams(
            collective_id=0, has_side_effects=True, vmem_limit_bytes=48 * 2**20
        ),
        cost_estimate=pl.CostEstimate(
            flops=2 * pairs * 64 * BLOCK * BLOCK,
            bytes_accessed=2 * 64 * (sb + tb) * BLOCK,
            transcendentals=2 * ITERS * pairs * BLOCK * BLOCK,
        ),
    )(
        ids, ids.reshape(1, pairs), ids.reshape(pairs, 1), source_cells, target_cells,
        source_logmass.reshape(sb, BLOCK), target_logmass.reshape(tb, BLOCK),
    )
    return f.reshape(-1), g.reshape(-1)


def solution(mesh):
    placed = (P(None, "rows"), P(None, "cols"), P("rows"), P("cols"), P("rows", None))
    body = functools.partial(on_device, mesh.shape["rows"], mesh.shape["cols"])
    return jax.shard_map(
        body, mesh=mesh, in_specs=placed, out_specs=(P("rows"), P("cols")), check_vma=False
    )
```

```python
import functools
import math

import jax
import jax.numpy as jnp
from jax import lax
from jax.experimental import pallas as pl
from jax.experimental.pallas import tpu as pltpu
from jax.sharding import PartitionSpec as P

BLOCK = 128
SUB = 8
LIST = 16
ITERS = 3
SLOTS = 4
EPS = 0.05
NEG = -1e30
LOG2E = math.log2(math.e)
UNIT = EPS / LOG2E
CHUNKS = 4
GROUPS = 8
SCAN = (1, 2, 4, 8, 16, 32)
UNROLL = 8
MESH = pl.DeviceIdType.MESH


def log2(v):
    return jnp.log(v) * LOG2E


def tree(op, parts):
    parts = list(parts)
    while len(parts) > 1:
        pairs = [op(p, q) for p, q in zip(parts[::2], parts[1::2])]
        parts = pairs + parts[len(parts) // 2 * 2 :]
    return parts[0]


def thirds(v):
    high = v.astype(jnp.bfloat16).astype(jnp.float32)
    rest = v - high
    middle = rest.astype(jnp.bfloat16).astype(jnp.float32)
    return [high, middle, rest - middle]


def pick(onehot, v):
    parts = [p.astype(jnp.bfloat16) for p in thirds(v)]
    out = jnp.dot(onehot, jnp.concatenate(parts, axis=1), preferred_element_type=jnp.float32)
    return (out[:, :BLOCK] + out[:, BLOCK : 2 * BLOCK]) + out[:, 2 * BLOCK :]


def kernel(
    n_rows, n_cols, remote,
    ids_ref, trow_ref, tcol_ref, x_hbm, y_hbm, a_hbm, b_hbm,
    f_ref, g_ref,
    x_ref, cells_y, a_ref, b_ref, tile, gam, sqx, sqy, phi1, hits, first, last, hot, spread, masks,
    peaks, sums, columns, src, trg, landing, own,
    x_sem, y_sem, src_send, src_recv, trg_send, trg_recv, own_send, own_recv,
):
    dim = x_hbm.shape[0]
    kappa = 2.0 * LOG2E / (dim * EPS)
    sb, tb = x_hbm.shape[1] // BLOCK, y_hbm.shape[1] // BLOCK
    pairs = sb * SLOTS
    share = tb // n_rows
    step = sb // CHUNKS
    group = tb // GROUPS
    if remote:
        me_r, me_c = lax.axis_index("rows"), lax.axis_index("cols")
        barrier = pltpu.get_barrier_semaphore()

        @pl.loop(1, n_rows)
        def _(d):
            pl.semaphore_signal(
                barrier, inc=1, device_id={"rows": lax.rem(me_r + d, n_rows)}, device_id_type=MESH
            )

        @pl.loop(1, n_cols)
        def _(d):
            pl.semaphore_signal(
                barrier, inc=1, device_id={"cols": lax.rem(me_c + d, n_cols)}, device_id_type=MESH
            )
    else:
        me_r = me_c = 0

    for n in range(GROUPS):

        @pl.loop(0, group, unroll=8)
        def _(k):
            t = n * group + k
            pltpu.make_async_copy(
                y_hbm.at[:, pl.ds(pl.multiple_of(t * BLOCK, BLOCK), BLOCK)],
                cells_y.at[t], y_sem.at[n],
            ).start()

    mass = b_hbm.at[pl.ds(pl.multiple_of(me_r * share, share), share)]
    fetch = [
        pltpu.make_async_copy(x_hbm, x_ref, x_sem.at[0]),
        pltpu.make_async_copy(a_hbm, a_ref, x_sem.at[1]),
        pltpu.make_async_copy(mass, b_ref, x_sem.at[2]),
    ]
    for copy in fetch:
        copy.start()

    tr, tc = trow_ref[...], tcol_ref[...]
    ip = lax.broadcasted_iota(jnp.int32, (pairs, pairs), 0)
    iq = lax.broadcasted_iota(jnp.int32, (pairs, pairs), 1)
    before = (tc < tr) | ((tc == tr) & (ip < iq))
    place = jnp.sum(jnp.where(before, 1.0, 0.0), axis=0, keepdims=True)
    put = place == ip.astype(jnp.float32)
    first[...] = jnp.where(put, 1.0, 0.0).astype(jnp.bfloat16)
    trf = tr.astype(jnp.float32)
    ordered = jnp.sum(jnp.where(put, trf, 0.0), axis=1, keepdims=True)
    it_ = lax.broadcasted_iota(jnp.int32, (tb, pairs), 0)
    iu = lax.broadcasted_iota(jnp.int32, (tb, pairs), 1)
    same = jnp.where(tr == it_, 1.0, 0.0)
    hot[...] = same.astype(jnp.bfloat16)
    upto = jnp.sum(jnp.where(tr <= it_, 1.0, 0.0), axis=1, keepdims=True)
    count = jnp.sum(same, axis=1, keepdims=True)
    at = jnp.where(count > 0.0, upto - 1.0, -1.0)
    last[...] = jnp.where(iu.astype(jnp.float32) == at, 1.0, 0.0).astype(jnp.bfloat16)
    hits[...] = jnp.broadcast_to(jnp.where(count > 0.0, 0.0, NEG), (tb, BLOCK))
    wide = jnp.broadcast_to(ordered, (pairs, BLOCK))
    rows = lax.broadcasted_iota(jnp.int32, (pairs, BLOCK), 0)
    for k, d in enumerate(SCAN):
        joined = (wide == pltpu.roll(wide, d, 0)) & (rows >= d)
        masks[k] = jnp.where(joined, 0.0, NEG)
    ik = lax.broadcasted_iota(jnp.int32, (BLOCK, step * BLOCK), 0)
    ib = lax.broadcasted_iota(jnp.int32, (BLOCK, step * BLOCK), 1) // BLOCK
    chosen = (ik == ib) | (ik == ib + step) | (ik == ib + 2 * step)
    spread[...] = jnp.where(chosen, 1.0, 0.0).astype(jnp.bfloat16)

    cells_y[tb] = jnp.zeros((dim, BLOCK), jnp.bfloat16)
    gam[pl.ds(tb, SUB), :] = jnp.full((SUB, BLOCK), NEG, jnp.float32)
    for n in range(GROUPS):
        landed = cells_y.at[pl.ds(n * group, group)]
        pltpu.make_async_copy(landed, landed, y_sem.at[n]).wait()

        @pl.loop(0, group, unroll=UNROLL)
        def _(k):
            t = n * group + k
            cells = cells_y[t].astype(jnp.float32)
            squares = jnp.sum(cells * cells, axis=0, keepdims=True) * (0.5 * kappa)
            sqy[pl.ds(t, 1), :] = squares
            gam[pl.ds(t, 1), :] = -squares

    for copy in fetch:
        copy.wait()

    @pl.loop(0, sb, unroll=UNROLL)
    def _(b):
        cells = x_ref[:, pl.ds(pl.multiple_of(b * BLOCK, BLOCK), BLOCK)].astype(jnp.float32)
        sqx[pl.ds(b, 1), :] = jnp.sum(cells * cells, axis=0, keepdims=True) * (0.5 * kappa)

    def send_rows(it, q):
        if remote:

            @pl.loop(1, n_cols)
            def _(d):
                there = src.at[it, me_c, pl.ds(q * step, step)]
                pltpu.make_async_remote_copy(
                    src_ref=there, dst_ref=there,
                    send_sem=src_send.at[it], recv_sem=src_recv.at[it, q],
                    device_id={"cols": lax.rem(me_c + d, n_cols)}, device_id_type=MESH,
                ).start()

    def rows_landed(it, q):
        if remote:
            landed = src.at[it, pl.ds(0, n_cols - 1), pl.ds(q * step, step)]
            pltpu.make_async_copy(landed, landed, src_recv.at[it, q]).wait()
        return src[it, :, pl.ds(q * step, step), :]

    def to_columns(v):
        parts = jnp.concatenate(
            thirds(v) + [jnp.zeros((BLOCK - 3 * step, BLOCK), jnp.float32)], axis=0
        )
        tall = parts.T.astype(jnp.bfloat16)
        for k in range(0, step, 2):
            both = jnp.dot(
                tall, spread[:, k * BLOCK : (k + 2) * BLOCK], preferred_element_type=jnp.float32
            )
            columns[k] = both[:, :BLOCK]
            columns[k + 1] = both[:, BLOCK:]

    def sum_rows(it, v, combine):
        trg[it] = v.reshape(n_rows, share, BLOCK)
        if remote:

            @pl.loop(1, n_rows)
            def _(d):
                peer = lax.rem(me_r + d, n_rows)
                pltpu.make_async_remote_copy(
                    src_ref=trg.at[it, peer], dst_ref=landing.at[it, me_r],
                    send_sem=trg_send.at[it], recv_sem=trg_recv.at[it],
                    device_id={"rows": peer}, device_id_type=MESH,
                ).start()

        landing[it, me_r] = trg[it, me_r]
        if remote:
            landed = landing.at[it, pl.ds(0, n_rows - 1)]
            pltpu.make_async_copy(landed, landed, trg_recv.at[it]).wait()
        own[it, me_r] = combine(landing[it])
        if remote:

            @pl.loop(1, n_rows)
            def _(d):
                pltpu.make_async_remote_copy(
                    src_ref=own.at[it, me_r], dst_ref=own.at[it, me_r],
                    send_sem=own_send.at[it], recv_sem=own_recv.at[it],
                    device_id={"rows": lax.rem(me_r + d, n_rows)}, device_id_type=MESH,
                ).start()

            landed = own.at[it, pl.ds(0, n_rows - 1)]
            pltpu.make_async_copy(landed, landed, own_recv.at[it]).wait()
        return own[it].reshape(tb, BLOCK)

    def strips(b, s):
        return [tile[b, r : r + SUB, s * BLOCK : (s + 1) * BLOCK] for r in range(0, BLOCK, SUB)]

    def column(k):
        return [columns[k, r : r + SUB, :] for r in range(0, BLOCK, SUB)]

    def place_at(p):
        return pl.ds(pl.multiple_of(p * SUB, SUB), SUB)

    def folded(ref):
        return [ref[pl.ds(k, pairs, stride=SUB), :] for k in range(SUB)]

    for q in range(CHUNKS):

        @pl.loop(0, step, unroll=UNROLL // 2)
        def _(k):
            b = q * step + k
            cells = x_ref[:, pl.ds(pl.multiple_of(b * BLOCK, BLOCK), BLOCK)]
            ids = [ids_ref[b * SLOTS + s] for s in range(SLOTS)]
            crossed = lax.dot_general(
                cells, jnp.concatenate([cells_y[t] for t in ids], axis=1), (((0,), (0,)), ((), ())),
                preferred_element_type=jnp.float32,
            )
            tile[b] = crossed * kappa
            starts = [gam[t][None, :] for t in ids]
            logs = []
            for r in range(0, BLOCK, 4 * SUB):
                scores = [
                    tile[b, r : r + 4 * SUB, s * BLOCK : (s + 1) * BLOCK] + starts[s]
                    for s in range(SLOTS)
                ]
                peak = tree(jnp.maximum, scores)
                logs.append(peak + log2(tree(jnp.add, [jnp.exp2(v - peak) for v in scores])))
            logs = jnp.concatenate(logs, axis=0).T
            peak = jnp.max(logs, axis=0, keepdims=True)
            total = jnp.sum(jnp.exp2(logs - peak), axis=0, keepdims=True)
            src[0, me_c, pl.ds(b, 1), :] = peak + log2(total)

        if remote and q == 0:
            pl.semaphore_wait(barrier, n_rows + n_cols - 2)
        send_rows(0, q)

    for q in range(CHUNKS):
        here = pl.ds(q * step, step)
        parts = rows_landed(0, q)
        peak = jnp.max(parts, axis=0)
        total = jnp.sum(jnp.exp2(parts - peak[None]), axis=0)
        phi = a_ref[here, :] * LOG2E - (peak + log2(total))
        phi1[here, :] = phi
        to_columns(phi)

        @pl.loop(0, step, unroll=UNROLL // 2)
        def _(k):
            b = q * step + k
            phis = column(k)
            for s in range(SLOTS):
                scores = [v + c for v, c in zip(strips(b, s), phis)]
                peak = tree(jnp.maximum, scores)
                exps = [jnp.exp2(v - peak) for v in scores]
                for r, e in enumerate(exps):
                    tile[b, r * SUB : (r + 1) * SUB, s * BLOCK : (s + 1) * BLOCK] = e
                peaks[place_at(b * SLOTS + s), :] = peak
                sums[place_at(b * SLOTS + s), :] = tree(jnp.add, exps)

    tops = folded(peaks)
    peak = tree(jnp.maximum, tops)
    total = tree(jnp.add, [v * jnp.exp2(p - peak) for v, p in zip(folded(sums), tops)])
    v = pick(first[...], peak + log2(total))
    for k, d in enumerate(SCAN):
        other = pltpu.roll(v, d, 0) + masks[k]
        peak = jnp.maximum(v, other)
        v = peak + log2(1.0 + jnp.exp2(jnp.minimum(v, other) - peak))

    def combine_logs(parts):
        peak = jnp.max(parts, axis=0)
        total = jnp.sum(jnp.exp2(parts - peak[None]), axis=0)
        return b_ref[...] * LOG2E - (peak + log2(total))

    gam[pl.ds(0, tb), :] = sum_rows(0, pick(last[...], v) + hits[...], combine_logs)

    @pl.loop(0, pairs, unroll=UNROLL)
    def _(p):
        peaks[place_at(p), :] = jnp.exp2(peaks[place_at(p), :] + gam[ids_ref[p]][None, :])

    gam[...] = jnp.ones(gam.shape, jnp.float32)

    lanes = lax.broadcasted_iota(jnp.int32, (BLOCK, BLOCK), 1)

    @pl.loop(1, ITERS)
    def _(it):
        for q in range(CHUNKS):

            def source_block(k, acc):
                b = q * step + k
                weights = [
                    peaks[place_at(b * SLOTS + s), :] * gam[ids_ref[b * SLOTS + s]][None, :]
                    for s in range(SLOTS)
                ]
                tiles = [strips(b, s) for s in range(SLOTS)]
                total = jnp.concatenate(
                    [
                        tree(jnp.add, [tiles[s][r] * weights[s] for s in range(SLOTS)])
                        for r in range(BLOCK // SUB)
                    ],
                    axis=0,
                )
                return jnp.where(lanes == k, jnp.sum(total, axis=1, keepdims=True), acc)

            acc = lax.fori_loop(
                0, step, source_block, jnp.zeros((BLOCK, BLOCK), jnp.float32), unroll=UNROLL
            )
            src[it, me_c, pl.ds(q * step, step), :] = acc.T[:step, :]
            send_rows(it, q)

        for q in range(CHUNKS):
            here = pl.ds(q * step, step)
            factor = jnp.exp(a_ref[here, :]) / jnp.sum(rows_landed(it, q), axis=0)
            f_ref[here, :] = UNIT * ((phi1[here, :] + sqx[here, :]) + log2(factor))
            to_columns(factor)

            @pl.loop(0, step, unroll=UNROLL)
            def _(k):
                b = q * step + k
                factors = column(k)
                for s in range(SLOTS):
                    total = tree(jnp.add, [v * c for v, c in zip(strips(b, s), factors)])
                    here = place_at(b * SLOTS + s)
                    sums[here, :] = total * peaks[here, :]

        gam[pl.ds(0, tb), :] = sum_rows(
            it,
            pick(hot[...], tree(jnp.add, folded(sums))),
            lambda parts: jnp.exp(b_ref[...]) / jnp.sum(parts, axis=0),
        )

    g_ref[...] = UNIT * ((own[0].reshape(tb, BLOCK) + sqy[...]) + log2(gam[pl.ds(0, tb), :]))
    if remote:
        for it in range(ITERS):
            sent = src.at[it, pl.ds(0, n_cols - 1)]
            pltpu.make_async_copy(sent, sent, src_send.at[it]).wait()
            sent = own.at[it, pl.ds(0, n_rows - 1)]
            pltpu.make_async_copy(sent, sent, own_send.at[it]).wait()
            pltpu.make_async_copy(sent, sent, trg_send.at[it]).wait()


def scratch(n_rows, n_cols, dim, sb, tb):
    f32, bf16, pairs = jnp.float32, jnp.bfloat16, sb * SLOTS
    dma = pltpu.SemaphoreType.DMA
    shared = (ITERS, n_rows, tb // n_rows, BLOCK)
    return [
        pltpu.VMEM((dim, sb * BLOCK), bf16),
        pltpu.VMEM((tb + 1, dim, BLOCK), bf16),
        pltpu.VMEM((sb, BLOCK), f32),
        pltpu.VMEM((tb // n_rows, BLOCK), f32),
        pltpu.VMEM((sb, BLOCK, SLOTS * BLOCK), f32),
        pltpu.VMEM((tb + SUB, BLOCK), f32),
        pltpu.VMEM((sb, BLOCK), f32),
        pltpu.VMEM((tb, BLOCK), f32),
        pltpu.VMEM((sb, BLOCK), f32),
        pltpu.VMEM((tb, BLOCK), f32),
        pltpu.VMEM((pairs, pairs), bf16),
        pltpu.VMEM((tb, pairs), bf16),
        pltpu.VMEM((tb, pairs), bf16),
        pltpu.VMEM((BLOCK, sb // CHUNKS * BLOCK), bf16),
        pltpu.VMEM((len(SCAN), pairs, BLOCK), f32),
        pltpu.VMEM((pairs * SUB, BLOCK), f32),
        pltpu.VMEM((pairs * SUB, BLOCK), f32),
        pltpu.VMEM((sb // CHUNKS, BLOCK, BLOCK), f32),
        pltpu.VMEM((ITERS, n_cols, sb, BLOCK), f32),
        pltpu.VMEM(shared, f32),
        pltpu.VMEM(shared, f32),
        pltpu.VMEM(shared, f32),
        dma((3,)),
        dma((GROUPS,)),
        dma((ITERS,)),
        dma((ITERS, CHUNKS)),
        dma((ITERS,)),
        dma((ITERS,)),
        dma((ITERS,)),
        dma((ITERS,)),
    ]


def make_call(n_rows, n_cols, dim, sb, tb, remote=True):
    pairs = sb * SLOTS
    vmem = pl.BlockSpec(memory_space=pltpu.VMEM)
    return pl.pallas_call(
        functools.partial(kernel, n_rows, n_cols, remote),
        out_shape=(
            jax.ShapeDtypeStruct((sb, BLOCK), jnp.float32),
            jax.ShapeDtypeStruct((tb, BLOCK), jnp.float32),
        ),
        in_specs=[pl.BlockSpec(memory_space=pltpu.SMEM), vmem, vmem]
        + [pl.BlockSpec(memory_space=pl.ANY)] * 4,
        out_specs=(vmem, vmem),
        scratch_shapes=scratch(n_rows, n_cols, dim, sb, tb),
        compiler_params=pltpu.CompilerParams(
            collective_id=0 if remote else None, has_side_effects=True, vmem_limit_bytes=48 * 2**20
        ),
        cost_estimate=pl.CostEstimate(
            flops=2 * pairs * dim * BLOCK * BLOCK,
            bytes_accessed=2 * dim * (sb + tb) * BLOCK,
            transcendentals=2 * pairs * BLOCK * BLOCK,
        ),
    )


def on_device(n_rows, n_cols, source_cells, target_cells, source_logmass, target_logmass, neighbours):
    sb = neighbours.shape[0]
    tb = target_cells.shape[1] // BLOCK
    pairs = sb * SLOTS
    local = neighbours - lax.axis_index("cols") * tb
    owned = (local >= 0) & (local < tb)
    upto = jnp.arange(LIST)[:, None] <= jnp.arange(LIST)[None, :]
    nth = jnp.sum(jnp.where(owned[:, :, None] & upto[None], 1, 0), axis=1)
    wanted = (nth[:, :, None] == 1 + jnp.arange(SLOTS)[None, None, :]) & owned[:, :, None]
    ids = tb + jnp.sum(jnp.where(wanted, local[:, :, None] - tb, 0), axis=1)
    ids = ids.reshape(pairs).astype(jnp.int32)
    f, g = make_call(n_rows, n_cols, source_cells.shape[0], sb, tb)(
        ids, ids.reshape(1, pairs), ids.reshape(pairs, 1), source_cells, target_cells,
        source_logmass.reshape(sb, BLOCK), target_logmass.reshape(tb, BLOCK),
    )
    return f.reshape(-1), g.reshape(-1)


def solution(mesh):
    placed = (P(None, "rows"), P(None, "cols"), P("rows"), P("cols"), P("rows", None))
    body = functools.partial(on_device, mesh.shape["rows"], mesh.shape["cols"])
    return jax.shard_map(
        body, mesh=mesh, in_specs=placed, out_specs=(P("rows"), P("cols")), check_vma=False
    )
```

```python
import functools
import math

import jax
import jax.numpy as jnp
from jax import lax
from jax.experimental import pallas as pl
from jax.experimental.pallas import tpu as pltpu
from jax.sharding import PartitionSpec as P

BLOCK = 128
SUB = 8
LIST = 16
ITERS = 3
SLOTS = 4
EPS = 0.05
NEG = -1e30
LOG2E = math.log2(math.e)
UNIT = EPS / LOG2E
CHUNKS = 4
GROUPS = 8
SCAN = (1, 2, 4, 8, 16, 32)
UNROLL = 16
MESH = pl.DeviceIdType.MESH


def log2(v):
    return jnp.log(v) * LOG2E


def tree(op, parts):
    parts = list(parts)
    while len(parts) > 1:
        pairs = [op(p, q) for p, q in zip(parts[::2], parts[1::2])]
        parts = pairs + parts[len(parts) // 2 * 2 :]
    return parts[0]


def thirds(v):
    high = v.astype(jnp.bfloat16).astype(jnp.float32)
    rest = v - high
    middle = rest.astype(jnp.bfloat16).astype(jnp.float32)
    return [high, middle, rest - middle]


def pick(onehot, v):
    parts = [p.astype(jnp.bfloat16) for p in thirds(v)]
    out = jnp.dot(onehot, jnp.concatenate(parts, axis=1), preferred_element_type=jnp.float32)
    return (out[:, :BLOCK] + out[:, BLOCK : 2 * BLOCK]) + out[:, 2 * BLOCK :]


def kernel(
    n_rows, n_cols, remote,
    x_hbm, y_hbm, a_hbm, b_hbm, n_hbm,
    f_ref, g_ref,
    n_ref, listed, ids_ref, x_ref, cells_y, a_ref, b_ref, tile, gam, sqx, sqy, phi1, hits, first, last,
    hot, masks, peaks, sums, src, trg, landing, own, x_sem, y_sem, src_send, src_recv, trg_send, trg_recv, own_send, own_recv,
):
    dim = x_hbm.shape[0]
    kappa = 2.0 * LOG2E / (dim * EPS)
    sb, tb = x_hbm.shape[1] // BLOCK, y_hbm.shape[1] // BLOCK
    pairs = sb * SLOTS
    share = tb // n_rows
    step = sb // CHUNKS
    group = tb // GROUPS
    if remote:
        me_r, me_c = lax.axis_index("rows"), lax.axis_index("cols")
        barrier = pltpu.get_barrier_semaphore()

        @pl.loop(1, n_rows)
        def _(d):
            pl.semaphore_signal(
                barrier, inc=1, device_id={"rows": lax.rem(me_r + d, n_rows)}, device_id_type=MESH
            )

        @pl.loop(1, n_cols)
        def _(d):
            pl.semaphore_signal(
                barrier, inc=1, device_id={"cols": lax.rem(me_c + d, n_cols)}, device_id_type=MESH
            )
    else:
        me_r = me_c = 0

    fetch_lists = pltpu.make_async_copy(n_hbm, n_ref, x_sem.at[3])
    fetch_lists.start()
    for n in range(GROUPS):

        @pl.loop(0, group, unroll=8)
        def _(k):
            t = n * group + k
            pltpu.make_async_copy(
                y_hbm.at[:, pl.ds(pl.multiple_of(t * BLOCK, BLOCK), BLOCK)],
                cells_y.at[t], y_sem.at[n],
            ).start()

    mass = b_hbm.at[pl.ds(pl.multiple_of(me_r * share, share), share)]
    fetch = [
        pltpu.make_async_copy(x_hbm, x_ref, x_sem.at[0]),
        pltpu.make_async_copy(a_hbm, a_ref, x_sem.at[1]),
        pltpu.make_async_copy(mass, b_ref, x_sem.at[2]),
    ]
    for copy in fetch:
        copy.start()

    fetch_lists.wait()
    local = n_ref[...] - me_c * tb
    owned = (local >= 0) & (local < tb)
    ik = lax.broadcasted_iota(jnp.int32, (LIST, LIST), 0)
    il = lax.broadcasted_iota(jnp.int32, (LIST, LIST), 1)
    nth = jnp.dot(
        jnp.where(owned, 1.0, 0.0).astype(jnp.bfloat16),
        jnp.where(ik <= il, 1.0, 0.0).astype(jnp.bfloat16),
        preferred_element_type=jnp.float32,
    )
    away = local.astype(jnp.float32) - tb
    slots = [
        jnp.sum(jnp.where(owned & (nth == s + 1.0), away, 0.0), axis=1, keepdims=True) + tb
        for s in range(SLOTS)
    ]
    at_lane = lax.broadcasted_iota(jnp.int32, (sb, BLOCK), 1)
    ids = sum(jnp.where(at_lane == s, slots[s], 0.0) for s in range(SLOTS)).astype(jnp.int32)
    listed[...] = jnp.minimum(jnp.maximum(ids, 0), tb)
    to_scalars = pltpu.make_async_copy(listed, ids_ref, x_sem.at[4])
    to_scalars.start()

    tc = jnp.concatenate(slots, axis=0)
    ip = lax.broadcasted_iota(jnp.int32, (pairs, pairs), 0)
    iq = lax.broadcasted_iota(jnp.int32, (pairs, pairs), 1)
    tr = jnp.sum(jnp.where(ip == iq, tc, 0.0), axis=0, keepdims=True)
    before = (tc < tr) | ((tc == tr) & (ip < iq))
    place = jnp.sum(jnp.where(before, 1.0, 0.0), axis=0, keepdims=True)
    put = place == ip.astype(jnp.float32)
    first[...] = jnp.where(put, 1.0, 0.0).astype(jnp.bfloat16)
    ordered = jnp.sum(jnp.where(put, tr, 0.0), axis=1, keepdims=True)
    it_ = lax.broadcasted_iota(jnp.int32, (tb, pairs), 0).astype(jnp.float32)
    iu = lax.broadcasted_iota(jnp.int32, (tb, pairs), 1)
    same = jnp.where(tr == it_, 1.0, 0.0)
    hot[...] = same.astype(jnp.bfloat16)
    upto = jnp.sum(jnp.where(tr <= it_, 1.0, 0.0), axis=1, keepdims=True)
    count = jnp.sum(same, axis=1, keepdims=True)
    at = jnp.where(count > 0.0, upto - 1.0, -1.0)
    last[...] = jnp.where(iu.astype(jnp.float32) == at, 1.0, 0.0).astype(jnp.bfloat16)
    hits[...] = jnp.broadcast_to(jnp.where(count > 0.0, 0.0, NEG), (tb, BLOCK))
    wide = jnp.broadcast_to(ordered, (pairs, BLOCK))
    rows = lax.broadcasted_iota(jnp.int32, (pairs, BLOCK), 0)
    for k, d in enumerate(SCAN):
        joined = (wide == pltpu.roll(wide, d, 0)) & (rows >= d)
        masks[k] = jnp.where(joined, 0.0, NEG)
    cells_y[tb] = jnp.zeros((dim, BLOCK), jnp.bfloat16)
    gam[pl.ds(tb, SUB), :] = jnp.full((SUB, BLOCK), NEG, jnp.float32)
    for n in range(GROUPS):
        landed = cells_y.at[pl.ds(n * group, group)]
        pltpu.make_async_copy(landed, landed, y_sem.at[n]).wait()

        @pl.loop(0, group, unroll=UNROLL)
        def _(k):
            t = n * group + k
            cells = cells_y[t].astype(jnp.float32)
            squares = jnp.sum(cells * cells, axis=0, keepdims=True) * (0.5 * kappa)
            sqy[pl.ds(t, 1), :] = squares
            gam[pl.ds(t, 1), :] = -squares

    for copy in fetch:
        copy.wait()

    @pl.loop(0, sb, unroll=UNROLL)
    def _(b):
        cells = x_ref[:, pl.ds(pl.multiple_of(b * BLOCK, BLOCK), BLOCK)].astype(jnp.float32)
        sqx[pl.ds(b, 1), :] = jnp.sum(cells * cells, axis=0, keepdims=True) * (0.5 * kappa)

    def chunk(q):
        return pl.ds(pl.multiple_of(q * step, step), step)

    def send_rows(it, q):
        if remote:

            @pl.loop(1, n_cols)
            def _(d):
                there = src.at[it, me_c, chunk(q)]
                pltpu.make_async_remote_copy(
                    src_ref=there, dst_ref=there,
                    send_sem=src_send.at[it], recv_sem=src_recv.at[it, q],
                    device_id={"cols": lax.rem(me_c + d, n_cols)}, device_id_type=MESH,
                ).start()

    def rows_landed(it, q):
        if remote:
            landed = src.at[it, pl.ds(0, n_cols - 1), chunk(q)]
            pltpu.make_async_copy(landed, landed, src_recv.at[it, q]).wait()
        return src[it, :, chunk(q), :]

    def to_columns(v):
        tall = jnp.concatenate([v, jnp.zeros((BLOCK - step, BLOCK), jnp.float32)], axis=0).T
        return [jnp.broadcast_to(tall[:, k : k + 1], (BLOCK, BLOCK)) for k in range(step)]

    def sum_rows(it, v, combine):
        trg[it] = v.reshape(n_rows, share, BLOCK)
        if remote:

            @pl.loop(1, n_rows)
            def _(d):
                peer = lax.rem(me_r + d, n_rows)
                pltpu.make_async_remote_copy(
                    src_ref=trg.at[it, peer], dst_ref=landing.at[it, me_r],
                    send_sem=trg_send.at[it], recv_sem=trg_recv.at[it],
                    device_id={"rows": peer}, device_id_type=MESH,
                ).start()

        landing[it, me_r] = trg[it, me_r]
        if remote:
            landed = landing.at[it, pl.ds(0, n_rows - 1)]
            pltpu.make_async_copy(landed, landed, trg_recv.at[it]).wait()
        own[it, me_r] = combine(landing[it])
        if remote:

            @pl.loop(1, n_rows)
            def _(d):
                pltpu.make_async_remote_copy(
                    src_ref=own.at[it, me_r], dst_ref=own.at[it, me_r],
                    send_sem=own_send.at[it], recv_sem=own_recv.at[it],
                    device_id={"rows": lax.rem(me_r + d, n_rows)}, device_id_type=MESH,
                ).start()

            landed = own.at[it, pl.ds(0, n_rows - 1)]
            pltpu.make_async_copy(landed, landed, own_recv.at[it]).wait()
        return own[it].reshape(tb, BLOCK)

    def strips(b, s):
        return [tile[b, r : r + SUB, s * BLOCK : (s + 1) * BLOCK] for r in range(0, BLOCK, SUB)]

    def cut(v):
        return [v[r : r + SUB, :] for r in range(0, BLOCK, SUB)]

    def place_at(p):
        return pl.ds(pl.multiple_of(p * SUB, SUB), SUB)

    def folded(ref):
        return [ref[pl.ds(k, pairs, stride=SUB), :] for k in range(SUB)]

    to_scalars.wait()

    @pl.loop(0, CHUNKS)
    def _(q):
        @pl.loop(0, step, unroll=UNROLL)
        def _(k):
            b = q * step + k
            cells = x_ref[:, pl.ds(pl.multiple_of(b * BLOCK, BLOCK), BLOCK)]
            ids = [ids_ref[b, s] for s in range(SLOTS)]
            crossed = lax.dot_general(
                cells, jnp.concatenate([cells_y[t] for t in ids], axis=1), (((0,), (0,)), ((), ())),
                preferred_element_type=jnp.float32,
            )
            crossed = crossed * kappa
            tile[b] = crossed
            starts = [gam[t][None, :] for t in ids]
            logs = []
            for r in range(0, BLOCK, 4 * SUB):
                scores = [
                    crossed[r : r + 4 * SUB, s * BLOCK : (s + 1) * BLOCK] + starts[s]
                    for s in range(SLOTS)
                ]
                peak = tree(jnp.maximum, scores)
                logs.append(peak + log2(tree(jnp.add, [jnp.exp2(v - peak) for v in scores])))
            logs = jnp.concatenate(logs, axis=0).T
            peak = jnp.max(logs, axis=0, keepdims=True)
            total = jnp.sum(jnp.exp2(logs - peak), axis=0, keepdims=True)
            src[0, me_c, pl.ds(b, 1), :] = peak + log2(total)

        if remote:

            @pl.when(q == 0)
            def _():
                pl.semaphore_wait(barrier, n_rows + n_cols - 2)

        send_rows(0, q)

    @pl.loop(0, CHUNKS)
    def _(q):
        here = chunk(q)
        parts = rows_landed(0, q)
        peak = jnp.max(parts, axis=0)
        total = jnp.sum(jnp.exp2(parts - peak[None]), axis=0)
        phi = a_ref[here, :] * LOG2E - (peak + log2(total))
        phi1[here, :] = phi
        for k, phis in enumerate(to_columns(phi)):
            b = q * step + k
            phis = cut(phis)
            for s in range(SLOTS):
                scores = [v + c for v, c in zip(strips(b, s), phis)]
                peak = tree(jnp.maximum, scores)
                exps = [jnp.exp2(v - peak) for v in scores]
                for r, e in enumerate(exps):
                    tile[b, r * SUB : (r + 1) * SUB, s * BLOCK : (s + 1) * BLOCK] = e
                peaks[place_at(s * sb + b), :] = peak
                sums[place_at(s * sb + b), :] = tree(jnp.add, exps)

    tops = folded(peaks)
    peak = tree(jnp.maximum, tops)
    total = tree(jnp.add, [v * jnp.exp2(p - peak) for v, p in zip(folded(sums), tops)])
    v = pick(first[...], peak + log2(total))
    for k, d in enumerate(SCAN):
        other = pltpu.roll(v, d, 0) + masks[k]
        peak = jnp.maximum(v, other)
        v = peak + log2(1.0 + jnp.exp2(jnp.minimum(v, other) - peak))

    def combine_logs(parts):
        peak = jnp.max(parts, axis=0)
        total = jnp.sum(jnp.exp2(parts - peak[None]), axis=0)
        return b_ref[...] * LOG2E - (peak + log2(total))

    gam[pl.ds(0, tb), :] = sum_rows(0, pick(last[...], v) + hits[...], combine_logs)

    lanes = lax.broadcasted_iota(jnp.int32, (BLOCK, BLOCK), 1)
    for it in range(1, ITERS):

        @pl.loop(0, CHUNKS)
        def _(q):
            def source_block(k, acc):
                b = q * step + k
                weights = []
                for s in range(SLOTS):
                    here = place_at(s * sb + b)
                    row = gam[ids_ref[b, s]][None, :]
                    if it == 1:
                        peaks[here, :] = jnp.exp2(peaks[here, :] + row)
                        weights.append(peaks[here, :])
                    else:
                        weights.append(peaks[here, :] * row)
                tiles = [strips(b, s) for s in range(SLOTS)]
                total = jnp.concatenate(
                    [
                        tree(jnp.add, [tiles[s][r] * weights[s] for s in range(SLOTS)])
                        for r in range(BLOCK // SUB)
                    ],
                    axis=0,
                )
                return jnp.where(lanes == k, jnp.sum(total, axis=1, keepdims=True), acc)

            acc = lax.fori_loop(
                0, step, source_block, jnp.zeros((BLOCK, BLOCK), jnp.float32), unroll=UNROLL
            )
            src[it, me_c, chunk(q), :] = acc.T[:step, :]
            send_rows(it, q)

        @pl.loop(0, CHUNKS)
        def _(q):
            here = chunk(q)
            factor = jnp.exp(a_ref[here, :]) / jnp.sum(rows_landed(it, q), axis=0)
            f_ref[here, :] = UNIT * ((phi1[here, :] + sqx[here, :]) + log2(factor))
            for k, factors in enumerate(to_columns(factor)):
                b = q * step + k
                factors = cut(factors)
                for s in range(SLOTS):
                    total = tree(jnp.add, [v * c for v, c in zip(strips(b, s), factors)])
                    pair = place_at(s * sb + b)
                    sums[pair, :] = total * peaks[pair, :]

        gam[pl.ds(0, tb), :] = sum_rows(
            it,
            pick(hot[...], tree(jnp.add, folded(sums))),
            lambda parts: jnp.exp(b_ref[...]) / jnp.sum(parts, axis=0),
        )

    g_ref[...] = UNIT * ((own[0].reshape(tb, BLOCK) + sqy[...]) + log2(gam[pl.ds(0, tb), :]))
    if remote:
        for it in range(ITERS):
            sent = src.at[it, pl.ds(0, n_cols - 1)]
            pltpu.make_async_copy(sent, sent, src_send.at[it]).wait()
            sent = own.at[it, pl.ds(0, n_rows - 1)]
            pltpu.make_async_copy(sent, sent, own_send.at[it]).wait()
            pltpu.make_async_copy(sent, sent, trg_send.at[it]).wait()


def scratch(n_rows, n_cols, dim, sb, tb):
    f32, bf16, pairs = jnp.float32, jnp.bfloat16, sb * SLOTS
    dma = pltpu.SemaphoreType.DMA
    shared = (ITERS, n_rows, tb // n_rows, BLOCK)
    return [
        pltpu.VMEM((sb, LIST), jnp.int32),
        pltpu.VMEM((sb, BLOCK), jnp.int32),
        pltpu.SMEM((sb, BLOCK), jnp.int32),
        pltpu.VMEM((dim, sb * BLOCK), bf16),
        pltpu.VMEM((tb + 1, dim, BLOCK), bf16),
        pltpu.VMEM((sb, BLOCK), f32),
        pltpu.VMEM((tb // n_rows, BLOCK), f32),
        pltpu.VMEM((sb, BLOCK, SLOTS * BLOCK), f32),
        pltpu.VMEM((tb + SUB, BLOCK), f32),
        pltpu.VMEM((sb, BLOCK), f32),
        pltpu.VMEM((tb, BLOCK), f32),
        pltpu.VMEM((sb, BLOCK), f32),
        pltpu.VMEM((tb, BLOCK), f32),
        pltpu.VMEM((pairs, pairs), bf16),
        pltpu.VMEM((tb, pairs), bf16),
        pltpu.VMEM((tb, pairs), bf16),
        pltpu.VMEM((len(SCAN), pairs, BLOCK), f32),
        pltpu.VMEM((pairs * SUB, BLOCK), f32),
        pltpu.VMEM((pairs * SUB, BLOCK), f32),
        pltpu.VMEM((ITERS, n_cols, sb, BLOCK), f32),
        pltpu.VMEM(shared, f32),
        pltpu.VMEM(shared, f32),
        pltpu.VMEM(shared, f32),
        dma((5,)),
        dma((GROUPS,)),
        dma((ITERS,)),
        dma((ITERS, CHUNKS)),
        dma((ITERS,)),
        dma((ITERS,)),
        dma((ITERS,)),
        dma((ITERS,)),
    ]


def make_call(n_rows, n_cols, dim, sb, tb, remote=True):
    pairs = sb * SLOTS
    vmem = pl.BlockSpec(memory_space=pltpu.VMEM)
    return pl.pallas_call(
        functools.partial(kernel, n_rows, n_cols, remote),
        out_shape=(
            jax.ShapeDtypeStruct((sb, BLOCK), jnp.float32),
            jax.ShapeDtypeStruct((tb, BLOCK), jnp.float32),
        ),
        in_specs=[pl.BlockSpec(memory_space=pltpu.HBM)] * 5,
        out_specs=(vmem, vmem),
        scratch_shapes=scratch(n_rows, n_cols, dim, sb, tb),
        compiler_params=pltpu.CompilerParams(
            collective_id=0 if remote else None, has_side_effects=True, vmem_limit_bytes=62 * 2**20
        ),
        cost_estimate=pl.CostEstimate(
            flops=2 * pairs * dim * BLOCK * BLOCK,
            bytes_accessed=2 * dim * (sb + tb) * BLOCK,
            transcendentals=2 * pairs * BLOCK * BLOCK,
        ),
    )


def on_device(n_rows, n_cols, source_cells, target_cells, source_logmass, target_logmass, neighbours):
    sb = neighbours.shape[0]
    tb = target_cells.shape[1] // BLOCK
    f, g = make_call(n_rows, n_cols, source_cells.shape[0], sb, tb)(
        source_cells, target_cells, source_logmass.reshape(sb, BLOCK),
        target_logmass.reshape(tb, BLOCK), neighbours,
    )
    return f.reshape(-1), g.reshape(-1)


def solution(mesh):
    placed = (P(None, "rows"), P(None, "cols"), P("rows"), P("cols"), P("rows", None))
    body = functools.partial(on_device, mesh.shape["rows"], mesh.shape["cols"])
    return jax.shard_map(
        body, mesh=mesh, in_specs=placed, out_specs=(P("rows"), P("cols")), check_vma=False
    )
```

```python
import functools
import math

import jax
import jax.numpy as jnp
from jax import lax
from jax.experimental import pallas as pl
from jax.experimental.pallas import tpu as pltpu
from jax.sharding import PartitionSpec as P

BLOCK = 128
SUB = 8
LIST = 16
ITERS = 3
SLOTS = 4
EPS = 0.05
NEG = -1e30
LOG2E = math.log2(math.e)
UNIT = EPS / LOG2E
CHUNKS = 4
ROW_NEAR = 4
COL_NEAR = 2
GROUPS = 8
SCAN = (1, 2, 4, 8, 16, 32)
UNROLL = 16
MESH = pl.DeviceIdType.MESH


def log2(v):
    return jnp.log(v) * LOG2E


def tree(op, parts):
    parts = list(parts)
    while len(parts) > 1:
        pairs = [op(p, q) for p, q in zip(parts[::2], parts[1::2])]
        parts = pairs + parts[len(parts) // 2 * 2 :]
    return parts[0]


def thirds(v):
    high = v.astype(jnp.bfloat16).astype(jnp.float32)
    rest = v - high
    middle = rest.astype(jnp.bfloat16).astype(jnp.float32)
    return [high, middle, rest - middle]


def swing(k, n):
    return n // 2 + (k + 1) // 2 * (1 - 2 * (k % 2))


def peer_of(k, me, n, near):
    far = n // near
    there = lax.rem(me // near + swing(k // near, far), far)
    return there * near + lax.rem(lax.rem(me, near) + swing(lax.rem(k, near), near), near)


def pick(onehot, v):
    parts = [p.astype(jnp.bfloat16) for p in thirds(v)]
    out = jnp.dot(onehot, jnp.concatenate(parts, axis=1), preferred_element_type=jnp.float32)
    return (out[:, :BLOCK] + out[:, BLOCK : 2 * BLOCK]) + out[:, 2 * BLOCK :]


def kernel(
    n_rows, n_cols, remote,
    x_hbm, y_hbm, a_hbm, b_hbm, n_hbm,
    f_ref, g_ref,
    n_ref, listed, ids_ref, x_ref, cells_y, a_ref, b_ref, tile, gam, sqx, sqy, phi1, hits, first, last,
    hot, masks, peaks, sums, src, trg, landing, own, x_sem, y_sem, src_send, src_recv, trg_send, trg_recv, own_send, own_recv,
):
    dim = x_hbm.shape[0]
    kappa = 2.0 * LOG2E / (dim * EPS)
    sb, tb = x_hbm.shape[1] // BLOCK, y_hbm.shape[1] // BLOCK
    pairs = sb * SLOTS
    share = tb // n_rows
    step = sb // CHUNKS
    group = tb // GROUPS
    if remote:
        me_r, me_c = lax.axis_index("rows"), lax.axis_index("cols")
        barrier = pltpu.get_barrier_semaphore()

        def row_peer(k):
            return {"rows": peer_of(k, me_r, n_rows, math.gcd(ROW_NEAR, n_rows))}

        def col_peer(k):
            return {"cols": peer_of(k, me_c, n_cols, math.gcd(COL_NEAR, n_cols))}

        @pl.loop(0, n_rows - 1)
        def _(k):
            pl.semaphore_signal(barrier, inc=1, device_id=row_peer(k), device_id_type=MESH)

        @pl.loop(0, n_cols - 1)
        def _(k):
            pl.semaphore_signal(barrier, inc=1, device_id=col_peer(k), device_id_type=MESH)

    else:
        me_r = me_c = 0

    fetch_lists = pltpu.make_async_copy(n_hbm, n_ref, x_sem.at[3])
    fetch_lists.start()
    for n in range(GROUPS):

        @pl.loop(0, group, unroll=8)
        def _(k):
            t = n * group + k
            pltpu.make_async_copy(
                y_hbm.at[:, pl.ds(pl.multiple_of(t * BLOCK, BLOCK), BLOCK)],
                cells_y.at[t], y_sem.at[n],
            ).start()

    mass = b_hbm.at[pl.ds(pl.multiple_of(me_r * share, share), share)]
    fetch = [
        pltpu.make_async_copy(x_hbm, x_ref, x_sem.at[0]),
        pltpu.make_async_copy(a_hbm, a_ref, x_sem.at[1]),
        pltpu.make_async_copy(mass, b_ref, x_sem.at[2]),
    ]
    for copy in fetch:
        copy.start()

    fetch_lists.wait()
    local = n_ref[...] - me_c * tb
    owned = (local >= 0) & (local < tb)
    ik = lax.broadcasted_iota(jnp.int32, (LIST, LIST), 0)
    il = lax.broadcasted_iota(jnp.int32, (LIST, LIST), 1)
    nth = jnp.dot(
        jnp.where(il <= ik, 1.0, 0.0).astype(jnp.bfloat16),
        jnp.where(owned, 1.0, 0.0).astype(jnp.bfloat16),
        preferred_element_type=jnp.float32,
    )
    away = local.astype(jnp.float32) - tb
    slots = [
        jnp.sum(jnp.where(owned & (nth == s + 1.0), away, 0.0), axis=0, keepdims=True) + tb
        for s in range(SLOTS)
    ]
    ids = jnp.concatenate(slots + [jnp.zeros((SUB - SLOTS, sb), jnp.float32)], axis=0)
    ids = jnp.concatenate([ids, jnp.zeros((SUB, BLOCK - sb), jnp.float32)], axis=1)
    listed[...] = jnp.minimum(jnp.maximum(ids.astype(jnp.int32), 0), tb)
    to_scalars = pltpu.make_async_copy(listed, ids_ref, x_sem.at[4])
    to_scalars.start()

    tr = jnp.concatenate(slots, axis=1)
    ip = lax.broadcasted_iota(jnp.int32, (pairs, pairs), 0)
    iq = lax.broadcasted_iota(jnp.int32, (pairs, pairs), 1)
    tc = jnp.sum(jnp.where(ip == iq, tr, 0.0), axis=1, keepdims=True)
    before = (tc < tr) | ((tc == tr) & (ip < iq))
    place = jnp.sum(jnp.where(before, 1.0, 0.0), axis=0, keepdims=True)
    put = place == ip.astype(jnp.float32)
    first[...] = jnp.where(put, 1.0, 0.0).astype(jnp.bfloat16)
    ordered = jnp.sum(jnp.where(put, tr, 0.0), axis=1, keepdims=True)
    it_ = lax.broadcasted_iota(jnp.int32, (tb, pairs), 0).astype(jnp.float32)
    iu = lax.broadcasted_iota(jnp.int32, (tb, pairs), 1)
    same = jnp.where(tr == it_, 1.0, 0.0)
    hot[...] = same.astype(jnp.bfloat16)
    upto = jnp.sum(jnp.where(tr <= it_, 1.0, 0.0), axis=1, keepdims=True)
    count = jnp.sum(same, axis=1, keepdims=True)
    at = jnp.where(count > 0.0, upto - 1.0, -1.0)
    last[...] = jnp.where(iu.astype(jnp.float32) == at, 1.0, 0.0).astype(jnp.bfloat16)
    hits[...] = jnp.broadcast_to(jnp.where(count > 0.0, 0.0, NEG), (tb, BLOCK))
    wide = jnp.broadcast_to(ordered, (pairs, BLOCK))
    rows = lax.broadcasted_iota(jnp.int32, (pairs, BLOCK), 0)
    for k, d in enumerate(SCAN):
        joined = (wide == pltpu.roll(wide, d, 0)) & (rows >= d)
        masks[k] = jnp.where(joined, 0.0, NEG)
    cells_y[tb] = jnp.zeros((dim, BLOCK), jnp.bfloat16)
    gam[pl.ds(tb, SUB), :] = jnp.full((SUB, BLOCK), NEG, jnp.float32)
    for n in range(GROUPS):
        landed = cells_y.at[pl.ds(n * group, group)]
        pltpu.make_async_copy(landed, landed, y_sem.at[n]).wait()

        @pl.loop(0, group, unroll=UNROLL)
        def _(k):
            t = n * group + k
            cells = cells_y[t].astype(jnp.float32)
            squares = jnp.sum(cells * cells, axis=0, keepdims=True) * (0.5 * kappa)
            sqy[pl.ds(t, 1), :] = squares
            gam[pl.ds(t, 1), :] = -squares

    for copy in fetch:
        copy.wait()

    def chunk(q):
        return pl.ds(pl.multiple_of(q * step, step), step)

    def send_rows(it, q):
        if remote:

            @pl.loop(0, n_cols - 1)
            def _(k):
                there = src.at[it, me_c, chunk(q)]
                pltpu.make_async_remote_copy(
                    src_ref=there, dst_ref=there,
                    send_sem=src_send.at[it], recv_sem=src_recv.at[it, q],
                    device_id=col_peer(k), device_id_type=MESH,
                ).start()

    def rows_landed(it, q):
        if remote:
            landed = src.at[it, pl.ds(0, n_cols - 1), chunk(q)]
            pltpu.make_async_copy(landed, landed, src_recv.at[it, q]).wait()
        return src[it, :, chunk(q), :]

    def to_columns(v):
        tall = jnp.concatenate([v, jnp.zeros((BLOCK - step, BLOCK), jnp.float32)], axis=0).T
        return [jnp.broadcast_to(tall[:, k : k + 1], (BLOCK, BLOCK)) for k in range(step)]

    def source_squares():
        @pl.loop(0, sb, unroll=UNROLL)
        def _(b):
            cells = x_ref[:, pl.ds(pl.multiple_of(b * BLOCK, BLOCK), BLOCK)].astype(jnp.float32)
            sqx[pl.ds(b, 1), :] = jnp.sum(cells * cells, axis=0, keepdims=True) * (0.5 * kappa)

    def sum_rows(it, v, combine):
        trg[it] = v.reshape(n_rows, share, BLOCK)
        if remote:

            @pl.loop(0, n_rows - 1)
            def _(k):
                peer = row_peer(k)
                pltpu.make_async_remote_copy(
                    src_ref=trg.at[it, peer["rows"]], dst_ref=landing.at[it, me_r],
                    send_sem=trg_send.at[it], recv_sem=trg_recv.at[it],
                    device_id=peer, device_id_type=MESH,
                ).start()

        if it == 0:
            source_squares()
        landing[it, me_r] = trg[it, me_r]
        if remote:
            landed = landing.at[it, pl.ds(0, n_rows - 1)]
            pltpu.make_async_copy(landed, landed, trg_recv.at[it]).wait()
        own[it, me_r] = combine(landing[it])
        if remote:

            @pl.loop(0, n_rows - 1)
            def _(k):
                pltpu.make_async_remote_copy(
                    src_ref=own.at[it, me_r], dst_ref=own.at[it, me_r],
                    send_sem=own_send.at[it], recv_sem=own_recv.at[it],
                    device_id=row_peer(k), device_id_type=MESH,
                ).start()

            landed = own.at[it, pl.ds(0, n_rows - 1)]
            pltpu.make_async_copy(landed, landed, own_recv.at[it]).wait()
        return own[it].reshape(tb, BLOCK)

    def strips(b, s):
        return [tile[b, r : r + SUB, s * BLOCK : (s + 1) * BLOCK] for r in range(0, BLOCK, SUB)]

    def cut(v):
        return [v[r : r + SUB, :] for r in range(0, BLOCK, SUB)]

    def place_at(p):
        return pl.ds(pl.multiple_of(p * SUB, SUB), SUB)

    def folded(ref):
        return [ref[pl.ds(k, pairs, stride=SUB), :] for k in range(SUB)]

    to_scalars.wait()

    @pl.loop(0, CHUNKS)
    def _(q):
        @pl.loop(0, step, unroll=UNROLL)
        def _(k):
            b = q * step + k
            cells = x_ref[:, pl.ds(pl.multiple_of(b * BLOCK, BLOCK), BLOCK)]
            ids = [ids_ref[s, b] for s in range(SLOTS)]
            crossed = lax.dot_general(
                cells, jnp.concatenate([cells_y[t] for t in ids], axis=1), (((0,), (0,)), ((), ())),
                preferred_element_type=jnp.float32,
            )
            crossed = crossed * kappa
            tile[b] = crossed
            starts = [gam[t][None, :] for t in ids]
            logs = []
            for r in range(0, BLOCK, 4 * SUB):
                scores = [
                    crossed[r : r + 4 * SUB, s * BLOCK : (s + 1) * BLOCK] + starts[s]
                    for s in range(SLOTS)
                ]
                peak = tree(jnp.maximum, scores)
                logs.append(peak + log2(tree(jnp.add, [jnp.exp2(v - peak) for v in scores])))
            logs = jnp.concatenate(logs, axis=0).T
            peak = jnp.max(logs, axis=0, keepdims=True)
            total = jnp.sum(jnp.exp2(logs - peak), axis=0, keepdims=True)
            src[0, me_c, pl.ds(b, 1), :] = peak + log2(total)

        if remote:

            @pl.when(q == 0)
            def _():
                pl.semaphore_wait(barrier, n_rows + n_cols - 2)

        send_rows(0, q)

    @pl.loop(0, CHUNKS)
    def _(q):
        here = chunk(q)
        parts = rows_landed(0, q)
        peak = jnp.max(parts, axis=0)
        total = jnp.sum(jnp.exp2(parts - peak[None]), axis=0)
        phi = a_ref[here, :] * LOG2E - (peak + log2(total))
        phi1[here, :] = phi
        for k, phis in enumerate(to_columns(phi)):
            b = q * step + k
            phis = cut(phis)
            for s in range(SLOTS):
                scores = [v + c for v, c in zip(strips(b, s), phis)]
                peak = tree(jnp.maximum, scores)
                exps = [jnp.exp2(v - peak) for v in scores]
                for r, e in enumerate(exps):
                    tile[b, r * SUB : (r + 1) * SUB, s * BLOCK : (s + 1) * BLOCK] = e
                peaks[place_at(s * sb + b), :] = peak
                sums[place_at(s * sb + b), :] = tree(jnp.add, exps)

    tops = folded(peaks)
    peak = tree(jnp.maximum, tops)
    total = tree(jnp.add, [v * jnp.exp2(p - peak) for v, p in zip(folded(sums), tops)])
    v = pick(first[...], peak + log2(total))
    for k, d in enumerate(SCAN):
        other = pltpu.roll(v, d, 0) + masks[k]
        peak = jnp.maximum(v, other)
        v = peak + log2(1.0 + jnp.exp2(jnp.minimum(v, other) - peak))

    def combine_logs(parts):
        peak = jnp.max(parts, axis=0)
        total = jnp.sum(jnp.exp2(parts - peak[None]), axis=0)
        return b_ref[...] * LOG2E - (peak + log2(total))

    gam[pl.ds(0, tb), :] = sum_rows(0, pick(last[...], v) + hits[...], combine_logs)

    lanes = lax.broadcasted_iota(jnp.int32, (BLOCK, BLOCK), 1)
    for it in range(1, ITERS):

        @pl.loop(0, CHUNKS)
        def _(q):
            def source_block(k, acc):
                b = q * step + k
                weights = []
                for s in range(SLOTS):
                    here = place_at(s * sb + b)
                    row = gam[ids_ref[s, b]][None, :]
                    if it == 1:
                        peaks[here, :] = jnp.exp2(peaks[here, :] + row)
                        weights.append(peaks[here, :])
                    else:
                        weights.append(peaks[here, :] * row)
                tiles = [strips(b, s) for s in range(SLOTS)]
                total = jnp.concatenate(
                    [
                        tree(jnp.add, [tiles[s][r] * weights[s] for s in range(SLOTS)])
                        for r in range(BLOCK // SUB)
                    ],
                    axis=0,
                )
                return jnp.where(lanes == k, jnp.sum(total, axis=1, keepdims=True), acc)

            acc = lax.fori_loop(
                0, step, source_block, jnp.zeros((BLOCK, BLOCK), jnp.float32), unroll=UNROLL
            )
            src[it, me_c, chunk(q), :] = acc.T[:step, :]
            send_rows(it, q)

        @pl.loop(0, CHUNKS)
        def _(q):
            here = chunk(q)
            factor = jnp.exp(a_ref[here, :]) / jnp.sum(rows_landed(it, q), axis=0)
            f_ref[here, :] = UNIT * ((phi1[here, :] + sqx[here, :]) + log2(factor))
            for k, factors in enumerate(to_columns(factor)):
                b = q * step + k
                factors = cut(factors)
                for s in range(SLOTS):
                    total = tree(jnp.add, [v * c for v, c in zip(strips(b, s), factors)])
                    pair = place_at(s * sb + b)
                    sums[pair, :] = total * peaks[pair, :]

        gam[pl.ds(0, tb), :] = sum_rows(
            it,
            pick(hot[...], tree(jnp.add, folded(sums))),
            lambda parts: jnp.exp(b_ref[...]) / jnp.sum(parts, axis=0),
        )

    g_ref[...] = UNIT * ((own[0].reshape(tb, BLOCK) + sqy[...]) + log2(gam[pl.ds(0, tb), :]))
    if remote:
        for it in range(ITERS):
            sent = src.at[it, pl.ds(0, n_cols - 1)]
            pltpu.make_async_copy(sent, sent, src_send.at[it]).wait()
            sent = own.at[it, pl.ds(0, n_rows - 1)]
            pltpu.make_async_copy(sent, sent, own_send.at[it]).wait()
            pltpu.make_async_copy(sent, sent, trg_send.at[it]).wait()


def scratch(n_rows, n_cols, dim, sb, tb):
    f32, bf16, pairs = jnp.float32, jnp.bfloat16, sb * SLOTS
    dma = pltpu.SemaphoreType.DMA
    shared = (ITERS, n_rows, tb // n_rows, BLOCK)
    return [
        pltpu.VMEM((LIST, sb), jnp.int32),
        pltpu.VMEM((SUB, BLOCK), jnp.int32),
        pltpu.SMEM((SUB, BLOCK), jnp.int32),
        pltpu.VMEM((dim, sb * BLOCK), bf16),
        pltpu.VMEM((tb + 1, dim, BLOCK), bf16),
        pltpu.VMEM((sb, BLOCK), f32),
        pltpu.VMEM((tb // n_rows, BLOCK), f32),
        pltpu.VMEM((sb, BLOCK, SLOTS * BLOCK), f32),
        pltpu.VMEM((tb + SUB, BLOCK), f32),
        pltpu.VMEM((sb, BLOCK), f32),
        pltpu.VMEM((tb, BLOCK), f32),
        pltpu.VMEM((sb, BLOCK), f32),
        pltpu.VMEM((tb, BLOCK), f32),
        pltpu.VMEM((pairs, pairs), bf16),
        pltpu.VMEM((tb, pairs), bf16),
        pltpu.VMEM((tb, pairs), bf16),
        pltpu.VMEM((len(SCAN), pairs, BLOCK), f32),
        pltpu.VMEM((pairs * SUB, BLOCK), f32),
        pltpu.VMEM((pairs * SUB, BLOCK), f32),
        pltpu.VMEM((ITERS, n_cols, sb, BLOCK), f32),
        pltpu.VMEM(shared, f32),
        pltpu.VMEM(shared, f32),
        pltpu.VMEM(shared, f32),
        dma((5,)),
        dma((GROUPS,)),
        dma((ITERS,)),
        dma((ITERS, CHUNKS)),
        dma((ITERS,)),
        dma((ITERS,)),
        dma((ITERS,)),
        dma((ITERS,)),
    ]


def make_call(n_rows, n_cols, dim, sb, tb, remote=True):
    pairs = sb * SLOTS
    vmem = pl.BlockSpec(memory_space=pltpu.VMEM)
    return pl.pallas_call(
        functools.partial(kernel, n_rows, n_cols, remote),
        out_shape=(
            pltpu.VMEM((sb, BLOCK), jnp.float32),
            pltpu.VMEM((tb, BLOCK), jnp.float32),
        ),
        in_specs=[pl.BlockSpec(memory_space=pltpu.HBM)] * 5,
        out_specs=(vmem, vmem),
        scratch_shapes=scratch(n_rows, n_cols, dim, sb, tb),
        compiler_params=pltpu.CompilerParams(
            collective_id=0 if remote else None, has_side_effects=True, vmem_limit_bytes=60 * 2**20
        ),
        cost_estimate=pl.CostEstimate(
            flops=2 * pairs * dim * BLOCK * BLOCK,
            bytes_accessed=2 * dim * (sb + tb) * BLOCK,
            transcendentals=2 * pairs * BLOCK * BLOCK,
        ),
    )


def on_device(n_rows, n_cols, source_cells, target_cells, source_logmass, target_logmass, neighbours):
    sb = neighbours.shape[0]
    tb = target_cells.shape[1] // BLOCK
    f, g = make_call(n_rows, n_cols, source_cells.shape[0], sb, tb)(
        source_cells, target_cells, source_logmass.reshape(sb, BLOCK),
        target_logmass.reshape(tb, BLOCK), neighbours.T,
    )
    return f.reshape(-1), g.reshape(-1)


def solution(mesh):
    placed = (P(None, "rows"), P(None, "cols"), P("rows"), P("cols"), P("rows", None))
    body = functools.partial(on_device, mesh.shape["rows"], mesh.shape["cols"])
    return jax.shard_map(
        body, mesh=mesh, in_specs=placed, out_specs=(P("rows"), P("cols")), check_vma=False
    )
```

```python
import functools
import math

import jax
import jax.numpy as jnp
from jax import lax
from jax.experimental import pallas as pl
from jax.experimental.pallas import tpu as pltpu
from jax.sharding import PartitionSpec as P

BLOCK = 128
SUB = 8
LIST = 16
ITERS = 3
SLOTS = 4
EPS = 0.05
NEG = -1e30
LOG2E = math.log2(math.e)
UNIT = EPS / LOG2E
CHUNKS = 4
ROW_NEAR = 4
COL_NEAR = 2
GROUPS = 8
SCAN = (1, 2, 4, 8, 16, 32)
UNROLL = 16
MESH = pl.DeviceIdType.MESH


def log2(v):
    return jnp.log(v) * LOG2E


def tree(op, parts):
    parts = list(parts)
    while len(parts) > 1:
        pairs = [op(p, q) for p, q in zip(parts[::2], parts[1::2])]
        parts = pairs + parts[len(parts) // 2 * 2 :]
    return parts[0]


def thirds(v):
    high = v.astype(jnp.bfloat16).astype(jnp.float32)
    rest = v - high
    middle = rest.astype(jnp.bfloat16).astype(jnp.float32)
    return [high, middle, rest - middle]


def swing(k, n):
    return n // 2 + (k + 1) // 2 * (1 - 2 * (k % 2))


def peer_of(k, me, n, near):
    far = n // near
    there = lax.rem(me // near + swing(k // near, far), far)
    return there * near + lax.rem(lax.rem(me, near) + swing(k % near, near), near)


def pick(onehot, v):
    parts = [p.astype(jnp.bfloat16) for p in thirds(v)]
    out = jnp.dot(onehot, jnp.concatenate(parts, axis=1), preferred_element_type=jnp.float32)
    return (out[:, :BLOCK] + out[:, BLOCK : 2 * BLOCK]) + out[:, 2 * BLOCK :]


def kernel(
    n_rows, n_cols, remote,
    x_hbm, y_hbm, a_hbm, b_hbm, n_hbm,
    f_ref, g_ref,
    n_ref, listed, ids_ref, x_ref, cells_y, a_ref, b_ref, tile, gam, sqx, sqy, phi1, hits, first, last,
    hot, masks, peaks, sums, src, trg, landing, own, x_sem, y_sem, src_send, src_recv, trg_send, trg_recv, own_send, own_recv,
):
    dim = x_hbm.shape[0]
    kappa = 2.0 * LOG2E / (dim * EPS)
    sb, tb = x_hbm.shape[1] // BLOCK, y_hbm.shape[1] // BLOCK
    pairs = sb * SLOTS
    share = tb // n_rows
    step = sb // CHUNKS
    group = tb // GROUPS
    if remote:
        me_r, me_c = lax.axis_index("rows"), lax.axis_index("cols")
        barrier = pltpu.get_barrier_semaphore()

        def row_peer(k):
            return {"rows": peer_of(k, me_r, n_rows, math.gcd(ROW_NEAR, n_rows))}

        def col_peer(k):
            return {"cols": peer_of(k, me_c, n_cols, math.gcd(COL_NEAR, n_cols))}

        @pl.loop(0, n_rows - 1)
        def _(k):
            pl.semaphore_signal(barrier, inc=1, device_id=row_peer(k), device_id_type=MESH)

        @pl.loop(0, n_cols - 1)
        def _(k):
            pl.semaphore_signal(barrier, inc=1, device_id=col_peer(k), device_id_type=MESH)

    else:
        me_r = me_c = 0

    fetch_lists = pltpu.make_async_copy(n_hbm, n_ref, x_sem.at[3])
    fetch_lists.start()
    for n in range(GROUPS):

        @pl.loop(0, group, unroll=8)
        def _(k):
            t = n * group + k
            pltpu.make_async_copy(
                y_hbm.at[:, pl.ds(pl.multiple_of(t * BLOCK, BLOCK), BLOCK)],
                cells_y.at[t], y_sem.at[n],
            ).start()

    mass = b_hbm.at[pl.ds(pl.multiple_of(me_r * share, share), share)]
    fetch = [
        pltpu.make_async_copy(x_hbm, x_ref, x_sem.at[0]),
        pltpu.make_async_copy(a_hbm, a_ref, x_sem.at[1]),
        pltpu.make_async_copy(mass, b_ref, x_sem.at[2]),
    ]
    for copy in fetch:
        copy.start()

    fetch_lists.wait()
    local = n_ref[...] - me_c * tb
    owned = (local >= 0) & (local < tb)
    ik = lax.broadcasted_iota(jnp.int32, (LIST, LIST), 0)
    il = lax.broadcasted_iota(jnp.int32, (LIST, LIST), 1)
    nth = jnp.dot(
        jnp.where(il <= ik, 1.0, 0.0).astype(jnp.bfloat16),
        jnp.where(owned, 1.0, 0.0).astype(jnp.bfloat16),
        preferred_element_type=jnp.float32,
    )
    away = local.astype(jnp.float32) - tb
    slots = [
        jnp.sum(jnp.where(owned & (nth == s + 1.0), away, 0.0), axis=0, keepdims=True) + tb
        for s in range(SLOTS)
    ]
    ids = jnp.concatenate(slots + [jnp.zeros((SUB - SLOTS, sb), jnp.float32)], axis=0)
    ids = jnp.concatenate([ids, jnp.zeros((SUB, BLOCK - sb), jnp.float32)], axis=1)
    listed[...] = jnp.minimum(jnp.maximum(ids.astype(jnp.int32), 0), tb)
    to_scalars = pltpu.make_async_copy(listed, ids_ref, x_sem.at[4])
    to_scalars.start()

    tr = jnp.concatenate(slots, axis=1)
    ip = lax.broadcasted_iota(jnp.int32, (pairs, pairs), 0)
    iq = lax.broadcasted_iota(jnp.int32, (pairs, pairs), 1)
    tc = jnp.sum(jnp.where(ip == iq, tr, 0.0), axis=1, keepdims=True)
    before = (tc < tr) | ((tc == tr) & (ip < iq))
    place = jnp.sum(jnp.where(before, 1.0, 0.0), axis=0, keepdims=True)
    put = place == ip.astype(jnp.float32)
    first[...] = jnp.where(put, 1.0, 0.0).astype(jnp.bfloat16)
    ordered = jnp.sum(jnp.where(put, tr, 0.0), axis=1, keepdims=True)
    it_ = lax.broadcasted_iota(jnp.int32, (tb, pairs), 0).astype(jnp.float32)
    iu = lax.broadcasted_iota(jnp.int32, (tb, pairs), 1)
    same = jnp.where(tr == it_, 1.0, 0.0)
    hot[...] = same.astype(jnp.bfloat16)
    upto = jnp.sum(jnp.where(tr <= it_, 1.0, 0.0), axis=1, keepdims=True)
    count = jnp.sum(same, axis=1, keepdims=True)
    at = jnp.where(count > 0.0, upto - 1.0, -1.0)
    last[...] = jnp.where(iu.astype(jnp.float32) == at, 1.0, 0.0).astype(jnp.bfloat16)
    hits[...] = jnp.broadcast_to(jnp.where(count > 0.0, 0.0, NEG), (tb, BLOCK))
    wide = jnp.broadcast_to(ordered, (pairs, BLOCK))
    rows = lax.broadcasted_iota(jnp.int32, (pairs, BLOCK), 0)
    for k, d in enumerate(SCAN):
        joined = (wide == pltpu.roll(wide, d, 0)) & (rows >= d)
        masks[k] = jnp.where(joined, 0.0, NEG)
    cells_y[tb] = jnp.zeros((dim, BLOCK), jnp.bfloat16)
    gam[pl.ds(tb, SUB), :] = jnp.full((SUB, BLOCK), NEG, jnp.float32)
    for n in range(GROUPS):
        landed = cells_y.at[pl.ds(n * group, group)]
        pltpu.make_async_copy(landed, landed, y_sem.at[n]).wait()

        @pl.loop(0, group, unroll=UNROLL)
        def _(k):
            t = n * group + k
            cells = cells_y[t].astype(jnp.float32)
            squares = jnp.sum(cells * cells, axis=0, keepdims=True) * (0.5 * kappa)
            sqy[pl.ds(t, 1), :] = squares
            gam[pl.ds(t, 1), :] = -squares

    for copy in fetch:
        copy.wait()

    def chunk(q):
        return pl.ds(pl.multiple_of(q * step, step), step)

    def send_rows(it, q):
        if remote:

            for k in range(n_cols - 1):
                there = src.at[it, me_c, chunk(q)]
                pltpu.make_async_remote_copy(
                    src_ref=there, dst_ref=there,
                    send_sem=src_send.at[it], recv_sem=src_recv.at[it, q],
                    device_id=col_peer(k), device_id_type=MESH,
                ).start()

    def rows_landed(it, q):
        if remote:
            landed = src.at[it, pl.ds(0, n_cols - 1), chunk(q)]
            pltpu.make_async_copy(landed, landed, src_recv.at[it, q]).wait()
        return src[it, :, chunk(q), :]

    def to_columns(v):
        tall = jnp.concatenate([v, jnp.zeros((BLOCK - step, BLOCK), jnp.float32)], axis=0).T
        return [jnp.broadcast_to(tall[:, k : k + 1], (BLOCK, BLOCK)) for k in range(step)]

    def source_squares():
        @pl.loop(0, sb, unroll=UNROLL)
        def _(b):
            cells = x_ref[:, pl.ds(pl.multiple_of(b * BLOCK, BLOCK), BLOCK)].astype(jnp.float32)
            sqx[pl.ds(b, 1), :] = jnp.sum(cells * cells, axis=0, keepdims=True) * (0.5 * kappa)

    def sum_rows(it, v, combine):
        trg[it] = v.reshape(n_rows, share, BLOCK)
        if remote:

            for k in range(n_rows - 1):
                peer = row_peer(k)
                pltpu.make_async_remote_copy(
                    src_ref=trg.at[it, peer["rows"]], dst_ref=landing.at[it, me_r],
                    send_sem=trg_send.at[it], recv_sem=trg_recv.at[it],
                    device_id=peer, device_id_type=MESH,
                ).start()

        if it == 0:
            source_squares()
        landing[it, me_r] = trg[it, me_r]
        if remote:
            landed = landing.at[it, pl.ds(0, n_rows - 1)]
            pltpu.make_async_copy(landed, landed, trg_recv.at[it]).wait()
        own[it, me_r] = combine(landing[it])
        if remote:

            for k in range(n_rows - 1):
                pltpu.make_async_remote_copy(
                    src_ref=own.at[it, me_r], dst_ref=own.at[it, me_r],
                    send_sem=own_send.at[it], recv_sem=own_recv.at[it],
                    device_id=row_peer(k), device_id_type=MESH,
                ).start()

            landed = own.at[it, pl.ds(0, n_rows - 1)]
            pltpu.make_async_copy(landed, landed, own_recv.at[it]).wait()
        return own[it].reshape(tb, BLOCK)

    def strips(b, s):
        return [tile[b, r : r + SUB, s * BLOCK : (s + 1) * BLOCK] for r in range(0, BLOCK, SUB)]

    def cut(v):
        return [v[r : r + SUB, :] for r in range(0, BLOCK, SUB)]

    def place_at(p):
        return pl.ds(pl.multiple_of(p * SUB, SUB), SUB)

    def folded(ref):
        return [ref[pl.ds(k, pairs, stride=SUB), :] for k in range(SUB)]

    to_scalars.wait()

    @pl.loop(0, CHUNKS)
    def _(q):
        @pl.loop(0, step, unroll=UNROLL)
        def _(k):
            b = q * step + k
            cells = x_ref[:, pl.ds(pl.multiple_of(b * BLOCK, BLOCK), BLOCK)]
            ids = [ids_ref[s, b] for s in range(SLOTS)]
            crossed = lax.dot_general(
                cells, jnp.concatenate([cells_y[t] for t in ids], axis=1), (((0,), (0,)), ((), ())),
                preferred_element_type=jnp.float32,
            )
            crossed = crossed * kappa
            tile[b] = crossed
            starts = [gam[t][None, :] for t in ids]
            logs = []
            for r in range(0, BLOCK, 4 * SUB):
                scores = [
                    crossed[r : r + 4 * SUB, s * BLOCK : (s + 1) * BLOCK] + starts[s]
                    for s in range(SLOTS)
                ]
                peak = tree(jnp.maximum, scores)
                logs.append(peak + log2(tree(jnp.add, [jnp.exp2(v - peak) for v in scores])))
            logs = jnp.concatenate(logs, axis=0).T
            peak = jnp.max(logs, axis=0, keepdims=True)
            total = jnp.sum(jnp.exp2(logs - peak), axis=0, keepdims=True)
            src[0, me_c, pl.ds(b, 1), :] = peak + log2(total)

        if remote:

            @pl.when(q == 0)
            def _():
                pl.semaphore_wait(barrier, n_rows + n_cols - 2)

        send_rows(0, q)

    @pl.loop(0, CHUNKS)
    def _(q):
        here = chunk(q)
        parts = rows_landed(0, q)
        peak = jnp.max(parts, axis=0)
        total = jnp.sum(jnp.exp2(parts - peak[None]), axis=0)
        phi = a_ref[here, :] * LOG2E - (peak + log2(total))
        phi1[here, :] = phi
        for k, phis in enumerate(to_columns(phi)):
            b = q * step + k
            phis = cut(phis)
            for s in range(SLOTS):
                scores = [v + c for v, c in zip(strips(b, s), phis)]
                peak = tree(jnp.maximum, scores)
                exps = [jnp.exp2(v - peak) for v in scores]
                for r, e in enumerate(exps):
                    tile[b, r * SUB : (r + 1) * SUB, s * BLOCK : (s + 1) * BLOCK] = e
                peaks[place_at(s * sb + b), :] = peak
                sums[place_at(s * sb + b), :] = tree(jnp.add, exps)

    tops = folded(peaks)
    peak = tree(jnp.maximum, tops)
    total = tree(jnp.add, [v * jnp.exp2(p - peak) for v, p in zip(folded(sums), tops)])
    v = pick(first[...], peak + log2(total))
    for k, d in enumerate(SCAN):
        other = pltpu.roll(v, d, 0) + masks[k]
        peak = jnp.maximum(v, other)
        v = peak + log2(1.0 + jnp.exp2(jnp.minimum(v, other) - peak))

    def combine_logs(parts):
        peak = jnp.max(parts, axis=0)
        total = jnp.sum(jnp.exp2(parts - peak[None]), axis=0)
        return b_ref[...] * LOG2E - (peak + log2(total))

    gam[pl.ds(0, tb), :] = sum_rows(0, pick(last[...], v) + hits[...], combine_logs)

    lanes = lax.broadcasted_iota(jnp.int32, (BLOCK, BLOCK), 1)
    for it in range(1, ITERS):

        @pl.loop(0, CHUNKS)
        def _(q):
            def source_block(k, acc):
                b = q * step + k
                weights = []
                for s in range(SLOTS):
                    here = place_at(s * sb + b)
                    row = gam[ids_ref[s, b]][None, :]
                    if it == 1:
                        peaks[here, :] = jnp.exp2(peaks[here, :] + row)
                        weights.append(peaks[here, :])
                    else:
                        weights.append(peaks[here, :] * row)
                tiles = [strips(b, s) for s in range(SLOTS)]
                total = jnp.concatenate(
                    [
                        tree(jnp.add, [tiles[s][r] * weights[s] for s in range(SLOTS)])
                        for r in range(BLOCK // SUB)
                    ],
                    axis=0,
                )
                return jnp.where(lanes == k, jnp.sum(total, axis=1, keepdims=True), acc)

            acc = lax.fori_loop(
                0, step, source_block, jnp.zeros((BLOCK, BLOCK), jnp.float32), unroll=UNROLL
            )
            src[it, me_c, chunk(q), :] = acc.T[:step, :]
            send_rows(it, q)

        @pl.loop(0, CHUNKS)
        def _(q):
            here = chunk(q)
            factor = jnp.exp(a_ref[here, :]) / jnp.sum(rows_landed(it, q), axis=0)
            f_ref[here, :] = UNIT * ((phi1[here, :] + sqx[here, :]) + log2(factor))
            for k, factors in enumerate(to_columns(factor)):
                b = q * step + k
                factors = cut(factors)
                for s in range(SLOTS):
                    total = tree(jnp.add, [v * c for v, c in zip(strips(b, s), factors)])
                    pair = place_at(s * sb + b)
                    sums[pair, :] = total * peaks[pair, :]

        gam[pl.ds(0, tb), :] = sum_rows(
            it,
            pick(hot[...], tree(jnp.add, folded(sums))),
            lambda parts: jnp.exp(b_ref[...]) / jnp.sum(parts, axis=0),
        )

    g_ref[...] = UNIT * ((own[0].reshape(tb, BLOCK) + sqy[...]) + log2(gam[pl.ds(0, tb), :]))
    if remote:
        for it in range(ITERS):
            sent = src.at[it, pl.ds(0, n_cols - 1)]
            pltpu.make_async_copy(sent, sent, src_send.at[it]).wait()
            sent = own.at[it, pl.ds(0, n_rows - 1)]
            pltpu.make_async_copy(sent, sent, own_send.at[it]).wait()
            pltpu.make_async_copy(sent, sent, trg_send.at[it]).wait()


def scratch(n_rows, n_cols, dim, sb, tb):
    f32, bf16, pairs = jnp.float32, jnp.bfloat16, sb * SLOTS
    dma = pltpu.SemaphoreType.DMA
    shared = (ITERS, n_rows, tb // n_rows, BLOCK)
    return [
        pltpu.VMEM((LIST, sb), jnp.int32),
        pltpu.VMEM((SUB, BLOCK), jnp.int32),
        pltpu.SMEM((SUB, BLOCK), jnp.int32),
        pltpu.VMEM((dim, sb * BLOCK), bf16),
        pltpu.VMEM((tb + 1, dim, BLOCK), bf16),
        pltpu.VMEM((sb, BLOCK), f32),
        pltpu.VMEM((tb // n_rows, BLOCK), f32),
        pltpu.VMEM((sb, BLOCK, SLOTS * BLOCK), f32),
        pltpu.VMEM((tb + SUB, BLOCK), f32),
        pltpu.VMEM((sb, BLOCK), f32),
        pltpu.VMEM((tb, BLOCK), f32),
        pltpu.VMEM((sb, BLOCK), f32),
        pltpu.VMEM((tb, BLOCK), f32),
        pltpu.VMEM((pairs, pairs), bf16),
        pltpu.VMEM((tb, pairs), bf16),
        pltpu.VMEM((tb, pairs), bf16),
        pltpu.VMEM((len(SCAN), pairs, BLOCK), f32),
        pltpu.VMEM((pairs * SUB, BLOCK), f32),
        pltpu.VMEM((pairs * SUB, BLOCK), f32),
        pltpu.VMEM((ITERS, n_cols, sb, BLOCK), f32),
        pltpu.VMEM(shared, f32),
        pltpu.VMEM(shared, f32),
        pltpu.VMEM(shared, f32),
        dma((5,)),
        dma((GROUPS,)),
        dma((ITERS,)),
        dma((ITERS, CHUNKS)),
        dma((ITERS,)),
        dma((ITERS,)),
        dma((ITERS,)),
        dma((ITERS,)),
    ]


def make_call(n_rows, n_cols, dim, sb, tb, remote=True):
    pairs = sb * SLOTS
    vmem = pl.BlockSpec(memory_space=pltpu.VMEM)
    return pl.pallas_call(
        functools.partial(kernel, n_rows, n_cols, remote),
        out_shape=(
            pltpu.VMEM((sb, BLOCK), jnp.float32),
            pltpu.VMEM((tb, BLOCK), jnp.float32),
        ),
        in_specs=[pl.BlockSpec(memory_space=pltpu.HBM)] * 5,
        out_specs=(vmem, vmem),
        scratch_shapes=scratch(n_rows, n_cols, dim, sb, tb),
        compiler_params=pltpu.CompilerParams(
            collective_id=0 if remote else None, has_side_effects=True, vmem_limit_bytes=60 * 2**20
        ),
        cost_estimate=pl.CostEstimate(
            flops=2 * pairs * dim * BLOCK * BLOCK,
            bytes_accessed=2 * dim * (sb + tb) * BLOCK,
            transcendentals=2 * pairs * BLOCK * BLOCK,
        ),
    )


def on_device(n_rows, n_cols, source_cells, target_cells, source_logmass, target_logmass, neighbours):
    sb = neighbours.shape[0]
    tb = target_cells.shape[1] // BLOCK
    f, g = make_call(n_rows, n_cols, source_cells.shape[0], sb, tb)(
        source_cells, target_cells, source_logmass.reshape(sb, BLOCK),
        target_logmass.reshape(tb, BLOCK), neighbours.T,
    )
    return f.reshape(-1), g.reshape(-1)


def solution(mesh):
    placed = (P(None, "rows"), P(None, "cols"), P("rows"), P("cols"), P("rows", None))
    body = functools.partial(on_device, mesh.shape["rows"], mesh.shape["cols"])
    return jax.shard_map(
        body, mesh=mesh, in_specs=placed, out_specs=(P("rows"), P("cols")), check_vma=False
    )
```

```python
import functools
import math

import jax
import jax.numpy as jnp
from jax import lax
from jax.experimental import pallas as pl
from jax.experimental.pallas import tpu as pltpu
from jax.sharding import PartitionSpec as P

BLOCK = 128
SUB = 8
LIST = 16
ITERS = 3
SLOTS = 4
EPS = 0.05
NEG = -1e30
LOG2E = math.log2(math.e)
UNIT = EPS / LOG2E
CHUNKS = 4
ROW_NEAR = 4
COL_NEAR = 2
GROUPS = 8
SCAN = (1, 2, 4, 8, 16, 32)
UNROLL = 16
MESH = pl.DeviceIdType.MESH


def log2(v):
    return jnp.log(v) * LOG2E


def tree(op, parts):
    parts = list(parts)
    while len(parts) > 1:
        pairs = [op(p, q) for p, q in zip(parts[::2], parts[1::2])]
        parts = pairs + parts[len(parts) // 2 * 2 :]
    return parts[0]


def thirds(v):
    high = v.astype(jnp.bfloat16).astype(jnp.float32)
    rest = v - high
    middle = rest.astype(jnp.bfloat16).astype(jnp.float32)
    return [high, middle, rest - middle]


def swing(k, n):
    return n // 2 + (k + 1) // 2 * (1 - 2 * (k % 2))


def peer_of(k, me, n, near):
    far = n // near
    if isinstance(k, int):
        away = [(i, j) for i in range(far) for j in range(near) if i or j]
        away.sort(key=lambda o: -min(o[0], far - o[0]) - min(o[1], near - o[1]))
        i, j = away[k]
        there = lax.rem(me // near + i, far)
        return there * near + lax.rem(lax.rem(me, near) + j, near)
    there = lax.rem(me // near + swing(k // near, far), far)
    return there * near + lax.rem(lax.rem(me, near) + swing(k % near, near), near)


def pick(onehot, v):
    parts = [p.astype(jnp.bfloat16) for p in thirds(v)]
    out = jnp.dot(onehot, jnp.concatenate(parts, axis=1), preferred_element_type=jnp.float32)
    return (out[:, :BLOCK] + out[:, BLOCK : 2 * BLOCK]) + out[:, 2 * BLOCK :]


def kernel(
    n_rows, n_cols, remote,
    x_hbm, y_hbm, a_hbm, b_hbm, n_hbm,
    f_ref, g_ref,
    n_ref, listed, ids_ref, x_ref, cells_y, a_ref, b_ref, tile, gam, sqx, sqy, phi1, hits, first, last,
    hot, masks, peaks, sums, src, trg, landing, own, x_sem, y_sem, src_send, src_recv, trg_send, trg_recv, own_send, own_recv,
):
    dim = x_hbm.shape[0]
    kappa = 2.0 * LOG2E / (dim * EPS)
    sb, tb = x_hbm.shape[1] // BLOCK, y_hbm.shape[1] // BLOCK
    pairs = sb * SLOTS
    share = tb // n_rows
    step = sb // CHUNKS
    group = tb // GROUPS
    if remote:
        me_r, me_c = lax.axis_index("rows"), lax.axis_index("cols")
        barrier = pltpu.get_barrier_semaphore()

        def row_peer(k):
            return {"rows": peer_of(k, me_r, n_rows, math.gcd(ROW_NEAR, n_rows))}

        def col_peer(k):
            return {"cols": peer_of(k, me_c, n_cols, math.gcd(COL_NEAR, n_cols))}

        @pl.loop(0, n_rows - 1)
        def _(k):
            pl.semaphore_signal(barrier, inc=1, device_id=row_peer(k), device_id_type=MESH)

        @pl.loop(0, n_cols - 1)
        def _(k):
            pl.semaphore_signal(barrier, inc=1, device_id=col_peer(k), device_id_type=MESH)

    else:
        me_r = me_c = 0

    fetch_lists = pltpu.make_async_copy(n_hbm, n_ref, x_sem.at[3])
    fetch_lists.start()
    for n in range(GROUPS):

        @pl.loop(0, group, unroll=8)
        def _(k):
            t = n * group + k
            pltpu.make_async_copy(
                y_hbm.at[:, pl.ds(pl.multiple_of(t * BLOCK, BLOCK), BLOCK)],
                cells_y.at[t], y_sem.at[n],
            ).start()

    mass = b_hbm.at[pl.ds(pl.multiple_of(me_r * share, share), share)]
    fetch = [
        pltpu.make_async_copy(x_hbm, x_ref, x_sem.at[0]),
        pltpu.make_async_copy(a_hbm, a_ref, x_sem.at[1]),
        pltpu.make_async_copy(mass, b_ref, x_sem.at[2]),
    ]
    for copy in fetch:
        copy.start()

    fetch_lists.wait()
    local = n_ref[...] - me_c * tb
    owned = (local >= 0) & (local < tb)
    ik = lax.broadcasted_iota(jnp.int32, (LIST, LIST), 0)
    il = lax.broadcasted_iota(jnp.int32, (LIST, LIST), 1)
    nth = jnp.dot(
        jnp.where(il <= ik, 1.0, 0.0).astype(jnp.bfloat16),
        jnp.where(owned, 1.0, 0.0).astype(jnp.bfloat16),
        preferred_element_type=jnp.float32,
    )
    away = local.astype(jnp.float32) - tb
    slots = [
        jnp.sum(jnp.where(owned & (nth == s + 1.0), away, 0.0), axis=0, keepdims=True) + tb
        for s in range(SLOTS)
    ]
    ids = jnp.concatenate(slots + [jnp.zeros((SUB - SLOTS, sb), jnp.float32)], axis=0)
    ids = jnp.concatenate([ids, jnp.zeros((SUB, BLOCK - sb), jnp.float32)], axis=1)
    listed[...] = jnp.minimum(jnp.maximum(ids.astype(jnp.int32), 0), tb)
    to_scalars = pltpu.make_async_copy(listed, ids_ref, x_sem.at[4])
    to_scalars.start()

    tr = jnp.concatenate(slots, axis=1)
    ip = lax.broadcasted_iota(jnp.int32, (pairs, pairs), 0)
    iq = lax.broadcasted_iota(jnp.int32, (pairs, pairs), 1)
    tc = jnp.sum(jnp.where(ip == iq, tr, 0.0), axis=1, keepdims=True)
    before = (tc < tr) | ((tc == tr) & (ip < iq))
    place = jnp.sum(jnp.where(before, 1.0, 0.0), axis=0, keepdims=True)
    put = place == ip.astype(jnp.float32)
    first[...] = jnp.where(put, 1.0, 0.0).astype(jnp.bfloat16)
    ordered = jnp.sum(jnp.where(put, tr, 0.0), axis=1, keepdims=True)
    it_ = lax.broadcasted_iota(jnp.int32, (tb, pairs), 0).astype(jnp.float32)
    iu = lax.broadcasted_iota(jnp.int32, (tb, pairs), 1)
    same = jnp.where(tr == it_, 1.0, 0.0)
    hot[...] = same.astype(jnp.bfloat16)
    upto = jnp.sum(jnp.where(tr <= it_, 1.0, 0.0), axis=1, keepdims=True)
    count = jnp.sum(same, axis=1, keepdims=True)
    at = jnp.where(count > 0.0, upto - 1.0, -1.0)
    last[...] = jnp.where(iu.astype(jnp.float32) == at, 1.0, 0.0).astype(jnp.bfloat16)
    hits[...] = jnp.broadcast_to(jnp.where(count > 0.0, 0.0, NEG), (tb, BLOCK))
    wide = jnp.broadcast_to(ordered, (pairs, BLOCK))
    rows = lax.broadcasted_iota(jnp.int32, (pairs, BLOCK), 0)
    for k, d in enumerate(SCAN):
        joined = (wide == pltpu.roll(wide, d, 0)) & (rows >= d)
        masks[k] = jnp.where(joined, 0.0, NEG)
    cells_y[tb] = jnp.zeros((dim, BLOCK), jnp.bfloat16)
    gam[pl.ds(tb, SUB), :] = jnp.full((SUB, BLOCK), NEG, jnp.float32)
    for n in range(GROUPS):
        landed = cells_y.at[pl.ds(n * group, group)]
        pltpu.make_async_copy(landed, landed, y_sem.at[n]).wait()

        @pl.loop(0, group, unroll=UNROLL)
        def _(k):
            t = n * group + k
            cells = cells_y[t].astype(jnp.float32)
            squares = jnp.sum(cells * cells, axis=0, keepdims=True) * (0.5 * kappa)
            sqy[pl.ds(t, 1), :] = squares
            gam[pl.ds(t, 1), :] = -squares

    for copy in fetch:
        copy.wait()

    def chunk(q):
        return pl.ds(pl.multiple_of(q * step, step), step)

    def send_rows(it, q):
        if remote:

            for k in range(n_cols - 1):
                there = src.at[it, me_c, chunk(q)]
                pltpu.make_async_remote_copy(
                    src_ref=there, dst_ref=there,
                    send_sem=src_send.at[it], recv_sem=src_recv.at[it, q],
                    device_id=col_peer(k), device_id_type=MESH,
                ).start()

    def rows_landed(it, q):
        if remote:
            landed = src.at[it, pl.ds(0, n_cols - 1), chunk(q)]
            pltpu.make_async_copy(landed, landed, src_recv.at[it, q]).wait()
        return src[it, :, chunk(q), :]

    def to_columns(v):
        tall = jnp.concatenate([v, jnp.zeros((BLOCK - step, BLOCK), jnp.float32)], axis=0).T
        return [jnp.broadcast_to(tall[:, k : k + 1], (BLOCK, BLOCK)) for k in range(step)]

    def source_squares():
        @pl.loop(0, sb, unroll=UNROLL)
        def _(b):
            cells = x_ref[:, pl.ds(pl.multiple_of(b * BLOCK, BLOCK), BLOCK)].astype(jnp.float32)
            sqx[pl.ds(b, 1), :] = jnp.sum(cells * cells, axis=0, keepdims=True) * (0.5 * kappa)

    def sum_rows(it, v, combine):
        trg[it] = v.reshape(n_rows, share, BLOCK)
        if remote:

            for k in range(n_rows - 1):
                peer = row_peer(k)
                pltpu.make_async_remote_copy(
                    src_ref=trg.at[it, peer["rows"]], dst_ref=landing.at[it, me_r],
                    send_sem=trg_send.at[it], recv_sem=trg_recv.at[it],
                    device_id=peer, device_id_type=MESH,
                ).start()

        if it == 0:
            source_squares()
        landing[it, me_r] = trg[it, me_r]
        if remote:
            landed = landing.at[it, pl.ds(0, n_rows - 1)]
            pltpu.make_async_copy(landed, landed, trg_recv.at[it]).wait()
        own[it, me_r] = combine(landing[it])
        if remote:

            for k in range(n_rows - 1):
                pltpu.make_async_remote_copy(
                    src_ref=own.at[it, me_r], dst_ref=own.at[it, me_r],
                    send_sem=own_send.at[it], recv_sem=own_recv.at[it],
                    device_id=row_peer(k), device_id_type=MESH,
                ).start()

            landed = own.at[it, pl.ds(0, n_rows - 1)]
            pltpu.make_async_copy(landed, landed, own_recv.at[it]).wait()
        return own[it].reshape(tb, BLOCK)

    def strips(b, s):
        return [tile[b, r : r + SUB, s * BLOCK : (s + 1) * BLOCK] for r in range(0, BLOCK, SUB)]

    def cut(v):
        return [v[r : r + SUB, :] for r in range(0, BLOCK, SUB)]

    def place_at(p):
        return pl.ds(pl.multiple_of(p * SUB, SUB), SUB)

    def folded(ref):
        return [ref[pl.ds(k, pairs, stride=SUB), :] for k in range(SUB)]

    to_scalars.wait()

    @pl.loop(0, CHUNKS)
    def _(q):
        @pl.loop(0, step, unroll=UNROLL)
        def _(k):
            b = q * step + k
            cells = x_ref[:, pl.ds(pl.multiple_of(b * BLOCK, BLOCK), BLOCK)]
            ids = [ids_ref[s, b] for s in range(SLOTS)]
            crossed = lax.dot_general(
                cells, jnp.concatenate([cells_y[t] for t in ids], axis=1), (((0,), (0,)), ((), ())),
                preferred_element_type=jnp.float32,
            )
            crossed = crossed * kappa
            tile[b] = crossed
            starts = [gam[t][None, :] for t in ids]
            logs = []
            for r in range(0, BLOCK, 4 * SUB):
                scores = [
                    crossed[r : r + 4 * SUB, s * BLOCK : (s + 1) * BLOCK] + starts[s]
                    for s in range(SLOTS)
                ]
                peak = tree(jnp.maximum, scores)
                logs.append(peak + log2(tree(jnp.add, [jnp.exp2(v - peak) for v in scores])))
            logs = jnp.concatenate(logs, axis=0).T
            peak = jnp.max(logs, axis=0, keepdims=True)
            total = jnp.sum(jnp.exp2(logs - peak), axis=0, keepdims=True)
            src[0, me_c, pl.ds(b, 1), :] = peak + log2(total)

        if remote:

            @pl.when(q == 0)
            def _():
                pl.semaphore_wait(barrier, n_rows + n_cols - 2)

        send_rows(0, q)

    @pl.loop(0, CHUNKS)
    def _(q):
        here = chunk(q)
        parts = rows_landed(0, q)
        peak = jnp.max(parts, axis=0)
        total = jnp.sum(jnp.exp2(parts - peak[None]), axis=0)
        phi = a_ref[here, :] * LOG2E - (peak + log2(total))
        phi1[here, :] = phi
        for k, phis in enumerate(to_columns(phi)):
            b = q * step + k
            phis = cut(phis)
            for s in range(SLOTS):
                scores = [v + c for v, c in zip(strips(b, s), phis)]
                peak = tree(jnp.maximum, scores)
                exps = [jnp.exp2(v - peak) for v in scores]
                for r, e in enumerate(exps):
                    tile[b, r * SUB : (r + 1) * SUB, s * BLOCK : (s + 1) * BLOCK] = e
                peaks[place_at(s * sb + b), :] = peak
                sums[place_at(s * sb + b), :] = tree(jnp.add, exps)

    tops = folded(peaks)
    peak = tree(jnp.maximum, tops)
    total = tree(jnp.add, [v * jnp.exp2(p - peak) for v, p in zip(folded(sums), tops)])
    v = pick(first[...], peak + log2(total))
    for k, d in enumerate(SCAN):
        other = pltpu.roll(v, d, 0) + masks[k]
        peak = jnp.maximum(v, other)
        v = peak + log2(1.0 + jnp.exp2(jnp.minimum(v, other) - peak))

    def combine_logs(parts):
        peak = jnp.max(parts, axis=0)
        total = jnp.sum(jnp.exp2(parts - peak[None]), axis=0)
        return b_ref[...] * LOG2E - (peak + log2(total))

    gam[pl.ds(0, tb), :] = sum_rows(0, pick(last[...], v) + hits[...], combine_logs)

    lanes = lax.broadcasted_iota(jnp.int32, (BLOCK, BLOCK), 1)
    for it in range(1, ITERS):

        @pl.loop(0, CHUNKS)
        def _(q):
            def source_block(k, acc):
                b = q * step + k
                weights = []
                for s in range(SLOTS):
                    here = place_at(s * sb + b)
                    row = gam[ids_ref[s, b]][None, :]
                    if it == 1:
                        peaks[here, :] = jnp.exp2(peaks[here, :] + row)
                        weights.append(peaks[here, :])
                    else:
                        weights.append(peaks[here, :] * row)
                tiles = [strips(b, s) for s in range(SLOTS)]
                total = jnp.concatenate(
                    [
                        tree(jnp.add, [tiles[s][r] * weights[s] for s in range(SLOTS)])
                        for r in range(BLOCK // SUB)
                    ],
                    axis=0,
                )
                return jnp.where(lanes == k, jnp.sum(total, axis=1, keepdims=True), acc)

            acc = lax.fori_loop(
                0, step, source_block, jnp.zeros((BLOCK, BLOCK), jnp.float32), unroll=UNROLL
            )
            src[it, me_c, chunk(q), :] = acc.T[:step, :]
            send_rows(it, q)

        @pl.loop(0, CHUNKS)
        def _(q):
            here = chunk(q)
            factor = jnp.exp(a_ref[here, :]) / jnp.sum(rows_landed(it, q), axis=0)
            f_ref[here, :] = UNIT * ((phi1[here, :] + sqx[here, :]) + log2(factor))
            for k, factors in enumerate(to_columns(factor)):
                b = q * step + k
                factors = cut(factors)
                for s in range(SLOTS):
                    total = tree(jnp.add, [v * c for v, c in zip(strips(b, s), factors)])
                    pair = place_at(s * sb + b)
                    sums[pair, :] = total * peaks[pair, :]

        gam[pl.ds(0, tb), :] = sum_rows(
            it,
            pick(hot[...], tree(jnp.add, folded(sums))),
            lambda parts: jnp.exp(b_ref[...]) / jnp.sum(parts, axis=0),
        )

    g_ref[...] = UNIT * ((own[0].reshape(tb, BLOCK) + sqy[...]) + log2(gam[pl.ds(0, tb), :]))
    if remote:
        for it in range(ITERS):
            sent = src.at[it, pl.ds(0, n_cols - 1)]
            pltpu.make_async_copy(sent, sent, src_send.at[it]).wait()
            sent = own.at[it, pl.ds(0, n_rows - 1)]
            pltpu.make_async_copy(sent, sent, own_send.at[it]).wait()
            pltpu.make_async_copy(sent, sent, trg_send.at[it]).wait()


def scratch(n_rows, n_cols, dim, sb, tb):
    f32, bf16, pairs = jnp.float32, jnp.bfloat16, sb * SLOTS
    dma = pltpu.SemaphoreType.DMA
    shared = (ITERS, n_rows, tb // n_rows, BLOCK)
    return [
        pltpu.VMEM((LIST, sb), jnp.int32),
        pltpu.VMEM((SUB, BLOCK), jnp.int32),
        pltpu.SMEM((SUB, BLOCK), jnp.int32),
        pltpu.VMEM((dim, sb * BLOCK), bf16),
        pltpu.VMEM((tb + 1, dim, BLOCK), bf16),
        pltpu.VMEM((sb, BLOCK), f32),
        pltpu.VMEM((tb // n_rows, BLOCK), f32),
        pltpu.VMEM((sb, BLOCK, SLOTS * BLOCK), f32),
        pltpu.VMEM((tb + SUB, BLOCK), f32),
        pltpu.VMEM((sb, BLOCK), f32),
        pltpu.VMEM((tb, BLOCK), f32),
        pltpu.VMEM((sb, BLOCK), f32),
        pltpu.VMEM((tb, BLOCK), f32),
        pltpu.VMEM((pairs, pairs), bf16),
        pltpu.VMEM((tb, pairs), bf16),
        pltpu.VMEM((tb, pairs), bf16),
        pltpu.VMEM((len(SCAN), pairs, BLOCK), f32),
        pltpu.VMEM((pairs * SUB, BLOCK), f32),
        pltpu.VMEM((pairs * SUB, BLOCK), f32),
        pltpu.VMEM((ITERS, n_cols, sb, BLOCK), f32),
        pltpu.VMEM(shared, f32),
        pltpu.VMEM(shared, f32),
        pltpu.VMEM(shared, f32),
        dma((5,)),
        dma((GROUPS,)),
        dma((ITERS,)),
        dma((ITERS, CHUNKS)),
        dma((ITERS,)),
        dma((ITERS,)),
        dma((ITERS,)),
        dma((ITERS,)),
    ]


def make_call(n_rows, n_cols, dim, sb, tb, remote=True):
    pairs = sb * SLOTS
    vmem = pl.BlockSpec(memory_space=pltpu.VMEM)
    return pl.pallas_call(
        functools.partial(kernel, n_rows, n_cols, remote),
        out_shape=(
            pltpu.VMEM((sb, BLOCK), jnp.float32),
            pltpu.VMEM((tb, BLOCK), jnp.float32),
        ),
        in_specs=[pl.BlockSpec(memory_space=pltpu.HBM)] * 5,
        out_specs=(vmem, vmem),
        scratch_shapes=scratch(n_rows, n_cols, dim, sb, tb),
        compiler_params=pltpu.CompilerParams(
            collective_id=0 if remote else None, has_side_effects=True, vmem_limit_bytes=60 * 2**20
        ),
        cost_estimate=pl.CostEstimate(
            flops=2 * pairs * dim * BLOCK * BLOCK,
            bytes_accessed=2 * dim * (sb + tb) * BLOCK,
            transcendentals=2 * pairs * BLOCK * BLOCK,
        ),
    )


def on_device(n_rows, n_cols, source_cells, target_cells, source_logmass, target_logmass, neighbours):
    sb = neighbours.shape[0]
    tb = target_cells.shape[1] // BLOCK
    f, g = make_call(n_rows, n_cols, source_cells.shape[0], sb, tb)(
        source_cells, target_cells, source_logmass.reshape(sb, BLOCK),
        target_logmass.reshape(tb, BLOCK), neighbours.T,
    )
    return f.reshape(-1), g.reshape(-1)


def solution(mesh):
    placed = (P(None, "rows"), P(None, "cols"), P("rows"), P("cols"), P("rows", None))
    body = functools.partial(on_device, mesh.shape["rows"], mesh.shape["cols"])
    return jax.shard_map(
        body, mesh=mesh, in_specs=placed, out_specs=(P("rows"), P("cols")), check_vma=False
    )
```
